512 devices in a mesh: rows: 64 (over z, x_hi, core), cols: 8 (over y, x_lo).
Axes of the slice: x: 4 (x_hi: 2, x_lo: 2; x = x_hi * 2 + x_lo), y: 4, z: 16, core: 2. Of those that a mesh axis runs over, the one named last changes fastest.
Arguments:
- atmosphere_variables: bfloat16 [2, 512, 256, 512], P(None, 'rows', 'cols'), may hold values from -24 to 24
- premix_gain_vector: float32 [512], replicated, may hold values from 0.5 to 1.5
- expand_weight: bfloat16 [512, 1024], replicated, may hold values from -0.25 to 0.25
- depth_weight: float32 [3, 3, 1024], replicated, may hold values from -2 to 2
- depth_bias: float32 [1024], replicated, may hold values from -3 to 3
- project_weight: bfloat16 [1024, 512], replicated, may hold values from -0.1875 to 0.1875
- norm_attn: float32 [512], replicated, may hold values from 0.5 to 1.5
- qkv_weight: bfloat16 [512, 1536], replicated, may hold values from -0.25 to 0.25
- out_weight: bfloat16 [512, 512], replicated, may hold values from -0.25 to 0.25
- bias_table: float32 [16, 15, 15], replicated, may hold values from -2 to 310
Outputs:
- mixed_fields: bfloat16 [2, 512, 256, 512], P(None, 'rows', 'cols')
The draws below stay inside these ranges and needn't reach their ends.
All inputs are finite; a program needn't handle non-finite values.
Results may differ from the reference program's by a relative error of at most 0.0052.
Values may be sent and summed in bfloat16 or wider, within the bound.
A program may use at most 64 MiB of HBM per device.

```python
import math
import jax
import jax.numpy as jnp
import numpy as np
from jax import lax

EMBED_DIMENSION = 512
HEADS = 16
INNER = 1024
PREDICTION_TOTAL = 2
CHART_NORTHWARD = 512
CHART_EASTWARD = 256


def draw_atmosphere_variables(key, part):
    key = jax.random.fold_in(key, 11)
    key_base, key_chan, lookup_element = jax.random.split(key, 3)
    complete_dimensions = (PREDICTION_TOTAL, CHART_NORTHWARD, CHART_EASTWARD, EMBED_DIMENSION)
    channel_scale = jnp.exp(jax.random.uniform(key_chan, (EMBED_DIMENSION,), jnp.float32, math.log(0.3), math.log(3.0)))
    element_multiplier = jnp.exp(jax.random.uniform(lookup_element, (PREDICTION_TOTAL, CHART_NORTHWARD, CHART_EASTWARD, 1), jnp.float32, math.log(0.3), math.log(3.0)))
    values = jax.random.normal(key_base, complete_dimensions, jnp.float32)
    return jnp.clip(values * channel_scale * element_multiplier, -24.0, 24.0).astype(jnp.bfloat16)


def draw_bias_table(key, part):
    key = jax.random.fold_in(key, 23)
    key_base = jax.random.fold_in(key, 0)
    table = jax.random.uniform(key_base, (HEADS, 15, 15), jnp.float32, -2.0, 2.0)
    return table


def normal_values(rng, dims, deviation, most, held_as=jnp.bfloat16):
    array = deviation * jax.random.normal(rng, dims, jnp.float32)
    return jnp.clip(array, min=-most, max=most).astype(held_as)


def setup_inputs(seed: int = 0) -> dict:
    key_list = jax.random.split(jax.random.key(seed), 11)
    return {
        "atmosphere_variables": draw_atmosphere_variables(jax.random.fold_in(key_list[10], 71), 0),
        "premix_gain_vector": jnp.clip(1.0 + 0.1 * jax.random.normal(key_list[1], (EMBED_DIMENSION,), jnp.float32), 0.5, 1.5),
        "expand_weight": normal_values(key_list[2], (EMBED_DIMENSION, INNER), EMBED_DIMENSION ** -0.5, 0.25),
        "depth_weight": normal_values(key_list[3], (3, 3, INNER), 9 ** -0.5, 2.0, jnp.float32),
        "depth_bias": normal_values(key_list[4], (INNER,), 0.5, 3.0, jnp.float32),
        "project_weight": normal_values(key_list[5], (INNER, EMBED_DIMENSION), INNER ** -0.5, 0.1875),
        "norm_attn": jnp.clip(1.0 + 0.1 * jax.random.normal(key_list[6], (EMBED_DIMENSION,), jnp.float32), 0.5, 1.5),
        "qkv_weight": normal_values(key_list[7], (EMBED_DIMENSION, 3 * EMBED_DIMENSION), EMBED_DIMENSION ** -0.5, 0.25),
        "out_weight": normal_values(key_list[8], (EMBED_DIMENSION, EMBED_DIMENSION), EMBED_DIMENSION ** -0.5, 0.25),
        "bias_table": draw_bias_table(jax.random.fold_in(key_list[10], 71), 0),
    }


def normalize_channels(values, gain_vector):
    average = lax.optimization_barrier(jnp.mean(values, axis=-1, keepdims=True))
    centred = values - average
    variance = lax.optimization_barrier(jnp.mean(centred * centred, axis=-1, keepdims=True))
    return centred * lax.rsqrt(variance + 1e-05) * gain_vector

def reference(atmosphere_variables, premix_gain_vector, expand_weight, depth_weight, depth_bias, project_weight, norm_attn, qkv_weight, out_weight, bias_table):
    map_height = atmosphere_variables.shape[1]
    map_width = atmosphere_variables.shape[2]
    embedding_dimension = atmosphere_variables.shape[3]
    expanded_channel_breadth = expand_weight.shape[1]
    head_count = bias_table.shape[0]
    head_size = embedding_dimension // head_count
    grid_side = 8
    member_ids = np.arange(grid_side * grid_side)
    row_of = member_ids // grid_side
    col_of = member_ids % grid_side
    row_delta = row_of[:, None] - row_of[None, :] + grid_side - 1
    col_delta = col_of[:, None] - col_of[None, :] + grid_side - 1
    position_bias = bias_table[:, row_delta, col_delta]
    scale_factor = head_size ** (-0.5)

    def prediction_unit_apply(lone_prediction):
        standardized = normalize_channels(lone_prediction.astype(jnp.float32), premix_gain_vector).astype(jnp.bfloat16)
        product = jnp.dot(standardized.reshape(-1, embedding_dimension), expand_weight, preferred_element_type=jnp.float32)
        expanded = jax.nn.gelu(product).astype(jnp.bfloat16).reshape(map_height, map_width, expanded_channel_breadth)
        padded = jnp.pad(expanded, ((1, 1), (1, 1), (0, 0)))
        filtered_fields = jnp.zeros((map_height, map_width, expanded_channel_breadth), jnp.float32)
        for row_tap in range(3):
            for col_tap in range(3):
                window = padded[row_tap:row_tap + map_height, col_tap:col_tap + map_width, :]
                filtered_fields = filtered_fields + window.astype(jnp.float32) * depth_weight[row_tap, col_tap]
        activated = jax.nn.gelu(filtered_fields + depth_bias).astype(jnp.bfloat16)
        residual_path = jnp.dot(activated.reshape(-1, expanded_channel_breadth), project_weight, preferred_element_type=jnp.float32)
        convolution_result = (lone_prediction.reshape(-1, embedding_dimension).astype(jnp.float32) + residual_path).astype(jnp.bfloat16)
        attention_input = normalize_channels(convolution_result.astype(jnp.float32), norm_attn).astype(jnp.bfloat16)
        groups = attention_input.reshape(grid_side, map_height // grid_side, grid_side, map_width // grid_side, embedding_dimension)
        groups = groups.transpose(1, 3, 0, 2, 4).reshape(-1, grid_side * grid_side, embedding_dimension)
        group_count = groups.shape[0]
        projected = jnp.dot(groups.reshape(-1, embedding_dimension), qkv_weight, preferred_element_type=jnp.float32)
        projected = projected.astype(jnp.bfloat16).reshape(group_count, grid_side * grid_side, 3, head_count, head_size)
        queries = projected[:, :, 0].astype(jnp.float32)
        keys_all = projected[:, :, 1].astype(jnp.float32)
        values_all = projected[:, :, 2].astype(jnp.float32)
        scores = jnp.einsum('gihd,gjhd->ghij', queries, keys_all) * scale_factor + position_bias[None]
        attention = jax.nn.softmax(scores, axis=-1).astype(jnp.bfloat16)
        context = jnp.einsum('ghij,gjhd->gihd', attention.astype(jnp.float32), values_all).astype(jnp.bfloat16)
        context = context.reshape(map_height // grid_side, map_width // grid_side, grid_side, grid_side, embedding_dimension)
        context = context.transpose(2, 0, 3, 1, 4).reshape(-1, embedding_dimension)
        attn_out = jnp.dot(context, out_weight, preferred_element_type=jnp.float32)
        blended_elements = (convolution_result.astype(jnp.float32) + attn_out).astype(jnp.bfloat16)
        return blended_elements.reshape(map_height, map_width, embedding_dimension)
    return lax.map(prediction_unit_apply, atmosphere_variables)
```

```python
import jax
import jax.numpy as jnp
from jax import lax
from jax.experimental import pallas as pl
from jax.experimental.pallas import tpu as pltpu
from jax.sharding import PartitionSpec as P

MESH = pl.DeviceIdType.MESH
F32 = jnp.float32
BF16 = jnp.bfloat16

FORECASTS = 2
ROWS = 8
COLS = 32
CELLS = ROWS * COLS
WIDTH = 512
INNER = 1024
SIDE = 8
PEERS = SIDE * SIDE
PIECE = 16
GROUPS = CELLS // PEERS
PADDED = 40
QUADS = 4


def gelu(v):
    half = 0.5 * v
    return half + half * jnp.tanh(v * (0.7978845608028654 + 0.035677408136300125 * (v * v)))


def layer_norm(v, gain):
    centred = v - jnp.mean(v, axis=-1, keepdims=True)
    variance = jnp.mean(centred * centred, axis=-1, keepdims=True)
    return centred * lax.rsqrt(variance + 1e-05) * gain


def iota(shape, dim):
    return lax.broadcasted_iota(jnp.int32, shape, dim)


def one_hot(condition):
    return jnp.where(condition, 1.0, 0.0).astype(BF16)


def matmul(a, b):
    return jnp.dot(a, b, preferred_element_type=F32)


def kernel(
    x_hbm, premix_ref, we_hbm, dw_ref, db_ref, wp_hbm, gain_ref, wqkv_hbm, wo_hbm, table_ref,
    out_hbm,
    xb, we, wp, wqkv, wo, edge, halo_rows, halo_edge, normed, ex, act, conv, pk,
    snd, rcv, bsnd, brcv, xg, qkv, flat, shifted, bias, ob,
    load_sem, halo_send, halo_recv, own_sem, fwd_send, fwd_recv, back_send, back_recv, out_sem,
):
    r = lax.axis_index("rows")
    c = lax.axis_index("cols")
    n_rows = lax.axis_size("rows")
    n_cols = lax.axis_size("cols")
    a, m = r // SIDE, r % SIDE
    me = a * SIDE + c

    loads = [
        pltpu.make_async_copy(src, dst, load_sem.at[i])
        for i, (src, dst) in enumerate(
            ((x_hbm, xb), (we_hbm, we), (wp_hbm, wp), (wqkv_hbm, wqkv), (wo_hbm, wo))
        )
    ]
    for load in loads:
        load.start()

    north, south = lax.rem(r + n_rows - 1, n_rows), lax.rem(r + 1, n_rows)
    west, east = lax.rem(c + n_cols - 1, n_cols), lax.rem(c + 1, n_cols)

    def peer(k):
        return lax.rem(a + k % SIDE, SIDE), lax.rem(c + k // SIDE, SIDE)

    barrier = pltpu.get_barrier_semaphore()
    for row, col in (
        (north, c), (south, c), (north, west), (north, east), (south, west), (south, east),
    ):
        pl.semaphore_signal(barrier, inc=1, device_id=(row, col), device_id_type=MESH)

    def greet(k, carry):
        pa, pc = peer(k)
        pl.semaphore_signal(barrier, inc=1, device_id=(pa * SIDE + m, pc), device_id_type=MESH)
        return carry

    lax.fori_loop(1, PEERS, greet, 0)

    loads[0].wait()
    place = iota((96, 512), 0)
    piece, index = place // 16, place % 16
    cell_f = jnp.where(piece < 2, index // 8, index % 2)
    cell_y = jnp.where(piece < 2, index % 8, jnp.where(piece < 4, 0, 7))
    cell_x = jnp.where(piece % 2 == 0, 0, 31)
    chosen = iota((96, 512), 1) == cell_f * CELLS + cell_y * COLS + cell_x
    edge[...] = matmul(one_hot(chosen), xb[...].reshape(512, WIDTH)).astype(BF16).reshape(6, 16, WIDTH)

    pl.semaphore_wait(barrier, PEERS - 1 + 6)

    def halo(i, src, dst, row, col):
        return pltpu.make_async_remote_copy(
            src_ref=src,
            dst_ref=dst,
            send_sem=halo_send.at[i],
            recv_sem=halo_recv.at[i],
            device_id=(row, col),
            device_id_type=MESH,
        )

    halos = [
        halo(0, xb.at[:, ROWS - 1], halo_rows.at[0], south, c),
        halo(1, xb.at[:, 0], halo_rows.at[1], north, c),
        halo(2, edge.at[0], halo_edge.at[0], r, west),
        halo(3, edge.at[1], halo_edge.at[1], r, east),
        halo(4, edge.at[5], halo_edge.at[2], south, east),
        halo(5, edge.at[4], halo_edge.at[3], south, west),
        halo(6, edge.at[3], halo_edge.at[4], north, east),
        halo(7, edge.at[2], halo_edge.at[5], north, west),
    ]
    for copy in halos:
        copy.start()

    def forward(f, k):
        pa, pc = peer(k)
        o = pa * SIDE + pc
        return pltpu.make_async_remote_copy(
            src_ref=snd.at[f, pl.ds(pl.multiple_of(o * PIECE, PIECE), PIECE)],
            dst_ref=rcv.at[f, pl.ds(pl.multiple_of(me * PIECE, PIECE), PIECE)],
            send_sem=fwd_send.at[f],
            recv_sem=fwd_recv.at[f],
            device_id=(pa * SIDE + m, pc),
            device_id_type=MESH,
        )

    def backward(f, k):
        pa, pc = peer(k)
        o = pa * SIDE + pc
        return pltpu.make_async_remote_copy(
            src_ref=bsnd.at[f, pl.ds(pl.multiple_of(o * PIECE, PIECE), PIECE)],
            dst_ref=brcv.at[f, pl.ds(pl.multiple_of(me * PIECE, PIECE), PIECE)],
            send_sem=back_send.at[f],
            recv_sem=back_recv.at[f],
            device_id=(pa * SIDE + m, pc),
            device_id_type=MESH,
        )

    def own(f, src, dst):
        mine = pl.ds(pl.multiple_of(me * PIECE, PIECE), PIECE)
        return pltpu.make_async_copy(src.at[f, mine], dst.at[f, mine], own_sem)

    def wait_all(f, ref, sem):
        others = ref.at[f, pl.ds(0, (PEERS - 1) * PIECE)]
        pltpu.make_async_copy(others, others, sem.at[f]).wait()

    premix = premix_ref[...]
    gain = gain_ref[...]

    def convolve(f, carry):
        def norm_rows(i, carry):
            v = xb[f, pl.ds(2 * i, 2)].astype(F32).reshape(64, WIDTH)
            normed[pl.ds(pl.multiple_of(i * 64, 64), 64)] = layer_norm(v, premix).astype(BF16)
            return carry

        lax.fori_loop(0, 4, norm_rows, 0)

        @pl.when(f == 0)
        def _():
            loads[1].wait()

        def expand_tile(i, carry):
            lanes = pl.ds(pl.multiple_of(i * 256, 256), 256)
            g = gelu(matmul(normed[0:CELLS], we[:, lanes])).astype(BF16).astype(F32)
            ex[1 : ROWS + 1, 0:COLS, lanes] = g.reshape(ROWS, COLS, 256)
            return carry

        lax.fori_loop(0, INNER // 256, expand_tile, 0)

        @pl.when(f == 0)
        def _():
            for copy in halos:
                copy.wait_recv()

        top = halo_rows[0, f].astype(F32) * jnp.where(r == 0, 0.0, 1.0)
        bottom = halo_rows[1, f].astype(F32) * jnp.where(r == n_rows - 1, 0.0, 1.0)
        normed[256:288] = layer_norm(top, premix).astype(BF16)
        normed[288:320] = layer_norm(bottom, premix).astype(BF16)
        place = iota((80, 96), 0)
        y, slot = place // 8, place % 8
        inside = ((y > 0) | (r > 0)) & ((y < 9) | (r < n_rows - 1))
        in_east = (slot == 0) & (c < n_cols - 1)
        in_west = (slot == 7) & (c > 0)
        source_east = jnp.where(y == 0, 48 + f, jnp.where(y == 9, 80 + f, f * 8 + y - 1))
        source_west = jnp.where(y == 0, 32 + f, jnp.where(y == 9, 64 + f, 16 + f * 8 + y - 1))
        source = jnp.where(in_east, source_east, source_west)
        chosen = (iota((80, 96), 1) == source) & inside & (in_east | in_west)
        sides = matmul(one_hot(chosen), halo_edge[...].reshape(96, WIDTH))
        normed[320:400] = layer_norm(sides, premix).astype(BF16)

        def expand_halo(i, carry):
            lanes = pl.ds(pl.multiple_of(i * 256, 256), 256)
            g = gelu(matmul(normed[CELLS:400], we[:, lanes])).astype(BF16).astype(F32)
            ex[0, 0:COLS, lanes] = g[0:32]
            ex[ROWS + 1, 0:COLS, lanes] = g[32:64]
            ex[:, COLS:PADDED, lanes] = g[64:144].reshape(ROWS + 2, 8, 256)
            return carry

        lax.fori_loop(0, INNER // 256, expand_halo, 0)

        def filter_row(y, carry):
            for i in range(INNER // 256):
                lanes = slice(i * 256, (i + 1) * 256)
                around = [ex[y + q, :, lanes] for q in range(3)]
                taps = [
                    sum(around[q] * dw_ref[q, s : s + 1, lanes] for q in range(3)) for s in range(3)
                ]
                total = (
                    pltpu.roll(taps[0], 1, 0) + taps[1] + pltpu.roll(taps[2], PADDED - 1, 0)
                )
                act[pl.ds(pl.multiple_of(y * COLS, COLS), COLS), lanes] = gelu(
                    total[0:COLS] + db_ref[:, lanes]
                ).astype(BF16)
            return carry

        lax.fori_loop(0, ROWS, filter_row, 0)

        @pl.when(f == 0)
        def _():
            loads[2].wait()

        for i in range(2):
            lanes = slice(i * 256, (i + 1) * 256)
            residual = xb[f, :, :, lanes].astype(F32).reshape(CELLS, 256)
            conv[f, :, lanes] = (residual + matmul(act[...], wp[:, lanes])).astype(BF16)

        def norm_out(i, carry):
            rows = pl.ds(pl.multiple_of(i * 64, 64), 64)
            v = layer_norm(conv[f, rows].astype(F32), gain)
            for q in range(4):
                pk[pl.ds(i * 256 + q, 64, stride=4), :] = v[:, q * 128 : (q + 1) * 128]
            return carry

        lax.fori_loop(0, 4, norm_out, 0)
        snd[f] = pk[...].astype(BF16)

        def send(k, carry):
            forward(f, k).start()
            return carry

        lax.fori_loop(1, PEERS, send, 0)
        copy = own(f, snd, rcv)
        copy.start()
        copy.wait()
        return carry

    lax.fori_loop(0, FORECASTS, convolve, 0)

    flat[...] = jnp.zeros_like(flat)
    total = jnp.zeros((16, 256), F32)
    for q in range(15):
        flat[:, 0:15] = table_ref[:, q, :]
        total = total + (pltpu.roll(flat[...], 16 * q, 1) if q else flat[...])
    flat[...] = total

    def shift(j, carry):
        moved = pltpu.roll(flat[...], 137 + 16 * (j // 8) + j % 8, 1)
        shifted[:, pl.ds(j, 1), :] = moved[:, 0:128].reshape(16, 1, 128)
        return carry

    lax.fori_loop(0, PEERS, shift, 0)
    source, target = iota((512, 256), 0), iota((512, 256), 1)
    member = target % 64
    spread = one_hot(source == (target // 64) * 128 + 16 * (member // 8) + member % 8)

    def set_bias(q, carry):
        rest = jnp.concatenate([shifted[q * 4 + h] for h in range(4)], axis=1)
        total = jnp.zeros((64, 256), F32)
        for _ in range(3):
            part = rest.astype(BF16)
            total = total + matmul(part, spread)
            rest = rest - part.astype(F32)
        bias[q] = total
        return carry

    lax.fori_loop(0, QUADS, set_bias, 0)
    loads[3].wait()

    head = iota((1, 128), 1) // 32
    own_lanes = [head == h for h in range(4)]

    def attend(f, carry):
        wait_all(f, rcv, fwd_recv)
        pk[...] = rcv[f].astype(F32)
        for t in range(GROUPS):
            for q in range(4):
                xg[t * 64 : (t + 1) * 64, q * 128 : (q + 1) * 128] = pk[
                    pl.ds(t * 4 + q, 64, stride=PIECE), :
                ].astype(BF16)

        def project(i, carry):
            lanes = pl.ds(pl.multiple_of(i * 256, 256), 256)
            qkv[:, lanes] = matmul(xg[...], wqkv[:, lanes]).astype(BF16)
            return carry

        lax.fori_loop(0, 6, project, 0)

        def group(t, carry):
            rows = pl.ds(pl.multiple_of(t * 64, 64), 64)
            for q in range(QUADS):
                lanes = slice(q * 128, (q + 1) * 128)
                query = qkv[rows, lanes]
                keys = qkv[rows, 512 + q * 128 : 640 + q * 128]
                values = qkv[rows, 1024 + q * 128 : 1152 + q * 128]
                apart = jnp.concatenate(
                    [query * one_hot(own_lanes[h]) for h in range(4)], axis=0
                )
                scores = lax.dot_general(
                    keys, apart, (((1,), (1,)), ((), ())), preferred_element_type=F32
                )
                scores = scores * (32**-0.5) + bias[q]
                powers = jnp.exp(scores - jnp.max(scores, axis=0, keepdims=True))
                share = 1.0 / jnp.sum(powers, axis=0, keepdims=True)
                attention = (powers * share).astype(BF16)
                mixed = lax.dot_general(
                    attention, values, (((0,), (0,)), ((), ())), preferred_element_type=F32
                )
                context = jnp.where(own_lanes[0], mixed[0:64], 0.0)
                for h in range(1, 4):
                    context = jnp.where(own_lanes[h], mixed[h * 64 : (h + 1) * 64], context)
                pk[pl.ds(t * 4 + q, 64, stride=PIECE), :] = context
            return carry

        lax.fori_loop(0, GROUPS, group, 0)
        bsnd[f] = pk[...].astype(BF16)

        def send(k, carry):
            backward(f, k).start()
            return carry

        lax.fori_loop(1, PEERS, send, 0)
        copy = own(f, bsnd, brcv)
        copy.start()
        copy.wait()
        return carry

    lax.fori_loop(0, FORECASTS, attend, 0)
    loads[4].wait()

    def finish(f, carry):
        wait_all(f, brcv, back_recv)
        pk[...] = brcv[f].astype(F32)
        for q in range(4):
            xg[:, q * 128 : (q + 1) * 128] = pk[pl.ds(q, CELLS, stride=4), :].astype(BF16)
        for i in range(2):
            lanes = slice(i * 256, (i + 1) * 256)
            total = conv[f, :, lanes].astype(F32) + matmul(xg[...], wo[:, lanes])
            ob[f, :, :, lanes] = total.astype(BF16).reshape(ROWS, COLS, 256)
        pltpu.make_async_copy(ob.at[f], out_hbm.at[f], out_sem.at[f]).start()
        return carry

    lax.fori_loop(0, FORECASTS, finish, 0)

    for copy in halos:
        copy.wait_send()
    for f in range(FORECASTS):
        wait_all(f, snd, fwd_send)
        wait_all(f, bsnd, back_send)
        pltpu.make_async_copy(ob.at[f], out_hbm.at[f], out_sem.at[f]).wait()


def on_device(
    atmosphere_variables,
    premix_gain_vector,
    expand_weight,
    depth_weight,
    depth_bias,
    project_weight,
    norm_attn,
    qkv_weight,
    out_weight,
    bias_table,
):
    whole = pl.BlockSpec(memory_space=pl.ANY)
    small = pl.BlockSpec(memory_space=pltpu.VMEM)
    tile = (FORECASTS, ROWS, COLS, WIDTH)
    pieces = (FORECASTS, PEERS * PIECE, 128)
    return pl.pallas_call(
        kernel,
        out_shape=jax.ShapeDtypeStruct(tile, BF16),
        in_specs=[whole, small, whole, small, small, whole, small, whole, whole, small],
        out_specs=whole,
        scratch_shapes=[
            pltpu.VMEM(tile, BF16),
            pltpu.VMEM((WIDTH, INNER), BF16),
            pltpu.VMEM((INNER, WIDTH), BF16),
            pltpu.VMEM((WIDTH, 3 * WIDTH), BF16),
            pltpu.VMEM((WIDTH, WIDTH), BF16),
            pltpu.VMEM((6, 16, WIDTH), BF16),
            pltpu.VMEM((2, FORECASTS, COLS, WIDTH), BF16),
            pltpu.VMEM((6, 16, WIDTH), BF16),
            pltpu.VMEM((400, WIDTH), BF16),
            pltpu.VMEM((ROWS + 2, PADDED, INNER), F32),
            pltpu.VMEM((CELLS, INNER), BF16),
            pltpu.VMEM((FORECASTS, CELLS, WIDTH), BF16),
            pltpu.VMEM((PEERS * PIECE, 128), F32),
            pltpu.VMEM(pieces, BF16),
            pltpu.VMEM(pieces, BF16),
            pltpu.VMEM(pieces, BF16),
            pltpu.VMEM(pieces, BF16),
            pltpu.VMEM((CELLS, WIDTH), BF16),
            pltpu.VMEM((CELLS, 3 * WIDTH), BF16),
            pltpu.VMEM((16, 256), F32),
            pltpu.VMEM((16, PEERS, 128), F32),
            pltpu.VMEM((QUADS, 64, 256), F32),
            pltpu.VMEM(tile, BF16),
            pltpu.SemaphoreType.DMA((5,)),
            pltpu.SemaphoreType.DMA((8,)),
            pltpu.SemaphoreType.DMA((8,)),
            pltpu.SemaphoreType.DMA,
            pltpu.SemaphoreType.DMA((FORECASTS,)),
            pltpu.SemaphoreType.DMA((FORECASTS,)),
            pltpu.SemaphoreType.DMA((FORECASTS,)),
            pltpu.SemaphoreType.DMA((FORECASTS,)),
            pltpu.SemaphoreType.DMA((FORECASTS,)),
        ],
        compiler_params=pltpu.CompilerParams(
            collective_id=0, has_side_effects=True, vmem_limit_bytes=40 * 1024 * 1024
        ),
        name="maxvit_layer",
    )(
        atmosphere_variables,
        premix_gain_vector.reshape(1, WIDTH),
        expand_weight,
        depth_weight,
        depth_bias.reshape(1, INNER),
        project_weight,
        norm_attn.reshape(1, WIDTH),
        qkv_weight,
        out_weight,
        bias_table,
    )


def solution(mesh):
    return jax.shard_map(
        on_device,
        mesh=mesh,
        in_specs=(P(None, "rows", "cols", None), P(), P(), P(), P(), P(), P(), P(), P(), P()),
        out_specs=P(None, "rows", "cols", None),
        check_vma=False,
    )
```

```python
import jax
import jax.numpy as jnp
from jax import lax
from jax.experimental import pallas as pl
from jax.experimental.pallas import tpu as pltpu
from jax.sharding import PartitionSpec as P

MESH = pl.DeviceIdType.MESH
F32 = jnp.float32
BF16 = jnp.bfloat16

FORECASTS = 2
ROWS = 8
COLS = 32
CELLS = ROWS * COLS
WIDTH = 512
INNER = 1024
SIDE = 8
PARTS = 4
PART_ROWS = FORECASTS * ROWS // PARTS
PART = PART_ROWS * COLS
PIECE = PART // SIDE
GROUPS = PIECE // SIDE
MEMBERS = SIDE * SIDE
PADDED = 40
QUADS = 4
LOG2E = 1.4426950408889634


def gelu(v):
    half = 0.5 * v
    return half + half * jnp.tanh(v * (0.7978845608028654 + 0.035677408136300125 * (v * v)))


def layer_norm(v, gain):
    centred = v - jnp.mean(v, axis=-1, keepdims=True)
    variance = jnp.mean(centred * centred, axis=-1, keepdims=True)
    return centred * lax.rsqrt(variance + 1e-05) * gain


def iota(shape, dim):
    return lax.broadcasted_iota(jnp.int32, shape, dim)


def one_hot(condition):
    return jnp.where(condition, 1.0, 0.0).astype(BF16)


def matmul(a, b):
    return jnp.dot(a, b, preferred_element_type=F32)


def kernel(
    x_hbm, premix_hbm, we_hbm, dw_hbm, db_hbm, wp_hbm, gain_hbm, wqkv_hbm, wo_hbm, table_hbm,
    out_hbm,
    xb, premix_ref, we, dw_ref, db_ref, wp, gain_ref, wqkv, wo, table_ref,
    edge, halo_rows, halo_edge, normed, ex, act, conv,
    att, mid, mid_out, owned, answers, mid_back, mid_return, returned,
    orders, xg, qkv, context, flat, shifted, bias, ob,
    load_sem, halo_send, halo_recv, sent, received, out_sem,
):
    r = lax.axis_index("rows")
    c = lax.axis_index("cols")
    n_rows = lax.axis_size("rows")
    n_cols = lax.axis_size("cols")
    a, m = r // SIDE, r % SIDE

    loads = [
        pltpu.make_async_copy(src, dst, load_sem.at[i])
        for i, (src, dst) in enumerate(
            (
                (x_hbm, xb), (premix_hbm, premix_ref), (we_hbm, we), (dw_hbm, dw_ref),
                (db_hbm, db_ref), (wp_hbm, wp), (gain_hbm, gain_ref), (table_hbm, table_ref),
                (wqkv_hbm, wqkv), (wo_hbm, wo),
            )
        )
    ]
    for load in loads[:3]:
        load.start()

    north, south = lax.rem(r + n_rows - 1, n_rows), lax.rem(r + 1, n_rows)
    west, east = lax.rem(c + n_cols - 1, n_cols), lax.rem(c + 1, n_cols)

    def along_rows(k):
        other = lax.rem(a + k, SIDE)
        return other, (other * SIDE + m, c)

    def along_cols(k):
        other = lax.rem(c + k, SIDE)
        return other, (r, other)

    barrier = pltpu.get_barrier_semaphore()
    for place in (
        (north, c), (south, c), (north, west), (north, east), (south, west), (south, east),
    ):
        pl.semaphore_signal(barrier, inc=1, device_id=place, device_id_type=MESH)

    def greet(k, carry):
        for along in (along_cols, along_rows):
            pl.semaphore_signal(barrier, inc=1, device_id=along(k)[1], device_id_type=MESH)
        return carry

    lax.fori_loop(1, SIDE, greet, 0)

    loads[0].wait()
    for load in loads[3:]:
        load.start()
    place = iota((96, 512), 0)
    piece, index = place // 16, place % 16
    cell_f = jnp.where(piece < 2, index // 8, index % 2)
    cell_y = jnp.where(piece < 2, index % 8, jnp.where(piece < 4, 0, 7))
    cell_x = jnp.where(piece % 2 == 0, 0, 31)
    chosen = iota((96, 512), 1) == cell_f * CELLS + cell_y * COLS + cell_x
    edge[...] = matmul(one_hot(chosen), xb[...].reshape(512, WIDTH)).astype(BF16).reshape(6, 16, WIDTH)

    pl.semaphore_wait(barrier, 2 * (SIDE - 1) + 6)

    def halo(i, src, dst, row, col):
        return pltpu.make_async_remote_copy(
            src_ref=src,
            dst_ref=dst,
            send_sem=halo_send.at[i],
            recv_sem=halo_recv.at[i],
            device_id=(row, col),
            device_id_type=MESH,
        )

    halos = [
        halo(0, xb.at[:, ROWS - 1], halo_rows.at[0], south, c),
        halo(1, xb.at[:, 0], halo_rows.at[1], north, c),
        halo(2, edge.at[0], halo_edge.at[0], r, west),
        halo(3, edge.at[1], halo_edge.at[1], r, east),
        halo(4, edge.at[5], halo_edge.at[2], south, east),
        halo(5, edge.at[4], halo_edge.at[3], south, west),
        halo(6, edge.at[3], halo_edge.at[4], north, east),
        halo(7, edge.at[2], halo_edge.at[5], north, west),
    ]
    for copy in halos:
        copy.start()

    def block(k):
        return pl.ds(pl.multiple_of(k * PIECE, PIECE), PIECE)

    def exchange(stage, p, src, dst, along, mine):
        def send(k, carry):
            other, place = along(k)
            pltpu.make_async_remote_copy(
                src_ref=src.at[p, block(other)],
                dst_ref=dst.at[p, block(mine)],
                send_sem=sent.at[stage, p],
                recv_sem=received.at[stage, p],
                device_id=place,
                device_id_type=MESH,
            ).start()
            return carry

        lax.fori_loop(1, SIDE, send, 0)
        dst[p, block(mine)] = src[p, block(mine)]

    def wait_all(ref, p, sem):
        others = ref.at[p, pl.ds(0, PART - PIECE)]
        pltpu.make_async_copy(others, others, sem).wait()

    loads[1].wait()
    premix = premix_ref[...]
    loads[2].wait()

    def expand_tile(f, carry):
        def norm_rows(i, carry):
            v = xb[f, pl.ds(2 * i, 2)].astype(F32).reshape(64, WIDTH)
            normed[pl.ds(pl.multiple_of(i * 64, 64), 64)] = layer_norm(v, premix).astype(BF16)
            return carry

        lax.fori_loop(0, 4, norm_rows, 0)

        def expand(i, carry):
            lanes = pl.ds(pl.multiple_of(i * 256, 256), 256)
            g = gelu(matmul(normed[0:CELLS], we[:, lanes])).astype(BF16).astype(F32)
            ex[f, 1 : ROWS + 1, 0:COLS, lanes] = g.reshape(ROWS, COLS, 256)
            return carry

        lax.fori_loop(0, INNER // 256, expand, 0)
        return carry

    lax.fori_loop(0, FORECASTS, expand_tile, 0)

    for copy in halos:
        copy.wait_recv()
    for load in loads[3:7]:
        load.wait()
    gain = gain_ref[...]

    def expand_halo(f):
        top = halo_rows[0, f].astype(F32) * jnp.where(r == 0, 0.0, 1.0)
        bottom = halo_rows[1, f].astype(F32) * jnp.where(r == n_rows - 1, 0.0, 1.0)
        normed[0:32] = layer_norm(top, premix).astype(BF16)
        normed[32:64] = layer_norm(bottom, premix).astype(BF16)
        place = iota((80, 96), 0)
        y, slot = place // 8, place % 8
        inside = ((y > 0) | (r > 0)) & ((y < 9) | (r < n_rows - 1))
        in_east = (slot == 0) & (c < n_cols - 1)
        in_west = (slot == 7) & (c > 0)
        source_east = jnp.where(y == 0, 48 + f, jnp.where(y == 9, 80 + f, f * 8 + y - 1))
        source_west = jnp.where(y == 0, 32 + f, jnp.where(y == 9, 64 + f, 16 + f * 8 + y - 1))
        source = jnp.where(in_east, source_east, source_west)
        chosen = (iota((80, 96), 1) == source) & inside & (in_east | in_west)
        sides = matmul(one_hot(chosen), halo_edge[...].reshape(96, WIDTH))
        normed[64:144] = layer_norm(sides, premix).astype(BF16)

        def expand(i, carry):
            lanes = pl.ds(pl.multiple_of(i * 256, 256), 256)
            g = gelu(matmul(normed[0:144], we[:, lanes])).astype(BF16).astype(F32)
            ex[f, 0, 0:COLS, lanes] = g[0:32]
            ex[f, ROWS + 1, 0:COLS, lanes] = g[32:64]
            ex[f, :, COLS:PADDED, lanes] = g[64:144].reshape(ROWS + 2, 8, 256)
            return carry

        lax.fori_loop(0, INNER // 256, expand, 0)

    def convolve(p, carry):
        f, first = p // 2, (p % 2) * PART_ROWS

        @pl.when(p % 2 == 0)
        def _():
            expand_halo(f)

        def filter_row(y, carry):
            for i in range(INNER // 256):
                lanes = slice(i * 256, (i + 1) * 256)
                around = [ex[f, first + y + q, :, lanes] for q in range(3)]
                taps = [
                    sum(around[q] * dw_ref[q, s : s + 1, lanes] for q in range(3)) for s in range(3)
                ]
                total = pltpu.roll(taps[0], 1, 0) + taps[1] + pltpu.roll(taps[2], PADDED - 1, 0)
                act[pl.ds(pl.multiple_of(y * COLS, COLS), COLS), lanes] = gelu(
                    total[0:COLS] + db_ref[:, lanes]
                ).astype(BF16)
            return carry

        lax.fori_loop(0, PART_ROWS, filter_row, 0)
        for i in range(2):
            lanes = slice(i * 256, (i + 1) * 256)
            residual = xb[f, pl.ds(first, PART_ROWS), :, lanes].astype(F32).reshape(PART, 256)
            conv[p, :, lanes] = (residual + matmul(act[...], wp[:, lanes])).astype(BF16)
        for i in range(2):
            rows = slice(i * 64, (i + 1) * 64)
            att[p, rows] = layer_norm(conv[p, rows].astype(F32), gain).astype(BF16)
        exchange(0, p, att, mid, along_rows, a)
        return carry

    lax.fori_loop(0, PARTS, convolve, 0)

    row, col = iota((PART, PART), 0), iota((PART, PART), 1)
    swapped = row // 16 * 2 + row % 16 // 2 * 16 + row % 2
    orders[0] = one_hot(col == swapped)
    grouped = row % 8 * 16 + row % 64 // 8 * 2 + row // 64
    orders[1] = one_hot(col == grouped)
    ungrouped = row % 2 * 64 + row % 16 // 2 * 8 + row // 16
    orders[2] = one_hot(col == ungrouped)

    def reorder(i, v):
        return matmul(orders[i], v).astype(BF16)

    def pass_on(p):
        wait_all(mid, p, received.at[0, p])
        mid_out[p] = reorder(0, mid[p])
        exchange(1, p, mid_out, owned, along_cols, c)

    pass_on(0)

    loads[7].wait()
    flat[...] = jnp.zeros_like(flat)
    total = jnp.zeros((16, 256), F32)
    for q in range(15):
        flat[:, 0:15] = table_ref[q]
        total = total + (pltpu.roll(flat[...], 16 * q, 1) if q else flat[...])
    flat[...] = total

    def shift(h, carry):
        row = jnp.broadcast_to(flat[pl.ds(h, 1), :], (8, 256))
        for i in range(SIDE):
            moved = pltpu.roll(row, 137 + 16 * i, 1, stride=1, stride_axis=0)
            shifted[h, i * 8 : (i + 1) * 8] = moved[:, 0:128]
        return carry

    lax.fori_loop(0, 16, shift, 0)
    source, target = iota((512, 256), 0), iota((512, 256), 1)
    member = target % 64
    spread = one_hot(source == (target // 64) * 128 + 16 * (member // 8) + member % 8)

    def set_bias(q, carry):
        rest = jnp.concatenate([shifted[q * 4 + h] for h in range(4)], axis=1)
        parts = []
        for _ in range(3):
            parts.append(rest.astype(BF16))
            rest = rest - parts[-1].astype(F32)
        total = matmul(jnp.concatenate(parts, axis=0), spread)
        bias[q] = (total[0:64] + total[64:128] + total[128:192]) * LOG2E
        return carry

    lax.fori_loop(0, QUADS, set_bias, 0)
    loads[8].wait()

    head = iota((1, 128), 1) // 32
    own_lanes = [head == h for h in range(4)]

    def attend(p, carry):
        wait_all(owned, p, received.at[1, p])
        xg[...] = reorder(1, owned[p])

        def project(i, carry):
            lanes = pl.ds(pl.multiple_of(i * 256, 256), 256)
            qkv[:, lanes] = matmul(xg[...], wqkv[:, lanes]).astype(BF16)
            return carry

        lax.fori_loop(0, 6, project, 0)

        for t in range(GROUPS):
            rows = slice(t * 64, (t + 1) * 64)
            for q in range(QUADS):
                lanes = slice(q * 128, (q + 1) * 128)
                query = qkv[rows, lanes]
                keys = qkv[rows, 512 + q * 128 : 640 + q * 128]
                values = qkv[rows, 1024 + q * 128 : 1152 + q * 128]
                apart = jnp.concatenate([query * one_hot(own_lanes[h]) for h in range(4)], axis=0)
                scores = lax.dot_general(
                    keys, apart, (((1,), (1,)), ((), ())), preferred_element_type=F32
                )
                scores = scores * (32**-0.5 * LOG2E) + bias[q]
                powers = jnp.exp2(scores - jnp.max(scores, axis=0, keepdims=True))
                share = 1.0 / jnp.sum(powers, axis=0, keepdims=True)
                attention = (powers * share).astype(BF16)
                mixed = lax.dot_general(
                    attention, values, (((0,), (0,)), ((), ())), preferred_element_type=F32
                )
                total = jnp.where(own_lanes[0], mixed[0:64], 0.0)
                for h in range(1, 4):
                    total = jnp.where(own_lanes[h], mixed[h * 64 : (h + 1) * 64], total)
                context[rows, lanes] = total.astype(BF16)

        answers[p] = reorder(2, context[...])
        exchange(2, p, answers, mid_back, along_cols, c)

        @pl.when(p < PARTS - 1)
        def _():
            pass_on(p + 1)

        wait_all(mid_back, p, received.at[2, p])
        mid_return[p] = reorder(0, mid_back[p])
        exchange(3, p, mid_return, returned, along_rows, a)
        return carry

    lax.fori_loop(0, PARTS, attend, 0)
    loads[9].wait()

    def written(p):
        f, first = p // 2, (p % 2) * PART_ROWS
        return pltpu.make_async_copy(
            ob.at[p], out_hbm.at[f, pl.ds(first, PART_ROWS)], out_sem.at[p]
        )

    def finish(p, carry):
        wait_all(returned, p, received.at[3, p])
        for i in range(2):
            lanes = slice(i * 256, (i + 1) * 256)
            total = conv[p, :, lanes].astype(F32) + matmul(returned[p], wo[:, lanes])
            ob[p, :, :, lanes] = total.astype(BF16).reshape(PART_ROWS, COLS, 256)
        written(p).start()
        return carry

    lax.fori_loop(0, PARTS, finish, 0)

    for copy in halos:
        copy.wait_send()

    def drain(p, carry):
        for stage, ref in enumerate((att, mid_out, answers, mid_return)):
            wait_all(ref, p, sent.at[stage, p])
        written(p).wait()
        return carry

    lax.fori_loop(0, PARTS, drain, 0)


def on_device(
    atmosphere_variables,
    premix_gain_vector,
    expand_weight,
    depth_weight,
    depth_bias,
    project_weight,
    norm_attn,
    qkv_weight,
    out_weight,
    bias_table,
):
    whole = pl.BlockSpec(memory_space=pltpu.HBM)
    tile = (FORECASTS, ROWS, COLS, WIDTH)
    parts = pltpu.VMEM((PARTS, PART, WIDTH), BF16)
    return pl.pallas_call(
        kernel,
        out_shape=jax.ShapeDtypeStruct(tile, BF16),
        in_specs=[whole] * 10,
        out_specs=pl.BlockSpec(memory_space=pl.ANY),
        scratch_shapes=[
            pltpu.VMEM(tile, BF16),
            pltpu.VMEM((1, WIDTH), F32),
            pltpu.VMEM((WIDTH, INNER), BF16),
            pltpu.VMEM((3, 3, INNER), F32),
            pltpu.VMEM((1, INNER), F32),
            pltpu.VMEM((INNER, WIDTH), BF16),
            pltpu.VMEM((1, WIDTH), F32),
            pltpu.VMEM((WIDTH, 3 * WIDTH), BF16),
            pltpu.VMEM((WIDTH, WIDTH), BF16),
            pltpu.VMEM((15, 16, 15), F32),
            pltpu.VMEM((6, 16, WIDTH), BF16),
            pltpu.VMEM((2, FORECASTS, COLS, WIDTH), BF16),
            pltpu.VMEM((6, 16, WIDTH), BF16),
            pltpu.VMEM((CELLS, WIDTH), BF16),
            pltpu.VMEM((FORECASTS, ROWS + 2, PADDED, INNER), F32),
            pltpu.VMEM((PART, INNER), BF16),
            *[parts] * 9,
            pltpu.VMEM((3, PART, PART), BF16),
            pltpu.VMEM((PART, WIDTH), BF16),
            pltpu.VMEM((PART, 3 * WIDTH), BF16),
            pltpu.VMEM((PART, WIDTH), BF16),
            pltpu.VMEM((16, 256), F32),
            pltpu.VMEM((16, MEMBERS, 128), F32),
            pltpu.VMEM((QUADS, MEMBERS, 256), F32),
            pltpu.VMEM((PARTS, PART_ROWS, COLS, WIDTH), BF16),
            pltpu.SemaphoreType.DMA((10,)),
            pltpu.SemaphoreType.DMA((8,)),
            pltpu.SemaphoreType.DMA((8,)),
            pltpu.SemaphoreType.DMA((4, PARTS)),
            pltpu.SemaphoreType.DMA((4, PARTS)),
            pltpu.SemaphoreType.DMA((PARTS,)),
        ],
        compiler_params=pltpu.CompilerParams(
            collective_id=0, has_side_effects=True, vmem_limit_bytes=56 * 1024 * 1024
        ),
        name="maxvit_layer",
    )(
        atmosphere_variables,
        premix_gain_vector.reshape(1, WIDTH),
        expand_weight,
        depth_weight,
        depth_bias.reshape(1, INNER),
        project_weight,
        norm_attn.reshape(1, WIDTH),
        qkv_weight,
        out_weight,
        bias_table.transpose(1, 0, 2),
    )


def solution(mesh):
    return jax.shard_map(
        on_device,
        mesh=mesh,
        in_specs=(P(None, "rows", "cols", None), P(), P(), P(), P(), P(), P(), P(), P(), P()),
        out_specs=P(None, "rows", "cols", None),
        check_vma=False,
    )
```

```python
import jax
import jax.numpy as jnp
from jax import lax
from jax.experimental import pallas as pl
from jax.experimental.pallas import tpu as pltpu
from jax.sharding import PartitionSpec as P

MESH = pl.DeviceIdType.MESH
F32 = jnp.float32
BF16 = jnp.bfloat16

FORECASTS = 2
ROWS = 8
COLS = 32
CELLS = ROWS * COLS
WIDTH = 512
INNER = 1024
SIDE = 8
PARTS = 4
PART = FORECASTS * CELLS // PARTS
INNER_ROWS = 5
PIECE = PART // SIDE
GROUPS = PIECE // SIDE
MEMBERS = SIDE * SIDE
PADDED = 40
QUADS = 4
LOG2E = 1.4426950408889634


def gelu(v):
    half = 0.5 * v
    return half + half * jnp.tanh(v * (0.7978845608028654 + 0.035677408136300125 * (v * v)))


def layer_norm(v, gain):
    centred = v - jnp.mean(v, axis=-1, keepdims=True)
    variance = jnp.mean(centred * centred, axis=-1, keepdims=True)
    return centred * lax.rsqrt(variance + 1e-05) * gain


def iota(shape, dim):
    return lax.broadcasted_iota(jnp.int32, shape, dim)


def one_hot(condition):
    return jnp.where(condition, 1.0, 0.0).astype(BF16)


def cells_of(inner, k):
    if inner:
        return (1 + k // 30) * COLS + 1 + k % 30
    edges = (1 + (k - 32) // 2) * COLS + (k - 32) % 2 * 31
    fifth = 5 * COLS + jnp.where(k == 40, 0, k - 32)
    last = 6 * COLS + k - 64
    return jnp.where(k < 32, k, jnp.where(k < 40, edges, jnp.where(k < 64, fifth, last)))


def matmul(a, b):
    return jnp.dot(a, b, preferred_element_type=F32)


def kernel(
    x_hbm, premix_hbm, we_hbm, dw_hbm, db_hbm, wp_hbm, gain_hbm, wqkv_hbm, wo_hbm, table_hbm,
    out_ref,
    xb, premix_ref, we, dw_ref, db_ref, wp, gain_ref, wqkv, wo, table_ref,
    edge, halo_rows, halo_edge, normed, ex, act, chosen_act, conv, choose, restore, finished,
    att, mid, mid_out, owned, answers, mid_back, mid_return, returned,
    orders, xg, qkv, context, flat, shifted, bias,
    load_sem, halo_send, halo_recv, sent, received,
):
    r = lax.axis_index("rows")
    c = lax.axis_index("cols")
    n_rows = lax.axis_size("rows")
    n_cols = lax.axis_size("cols")
    a, m = r // SIDE, r % SIDE

    loads = [
        pltpu.make_async_copy(src, dst, load_sem.at[i])
        for i, (src, dst) in enumerate(
            (
                (x_hbm.at[0], xb.at[0]), (premix_hbm, premix_ref), (we_hbm, we), (dw_hbm, dw_ref),
                (db_hbm, db_ref), (wp_hbm, wp), (gain_hbm, gain_ref), (table_hbm, table_ref),
                (wqkv_hbm, wqkv), (wo_hbm, wo), (x_hbm.at[1], xb.at[1]),
            )
        )
    ]
    for load in loads[:3] + loads[10:]:
        load.start()

    north, south = lax.rem(r + n_rows - 1, n_rows), lax.rem(r + 1, n_rows)
    west, east = lax.rem(c + n_cols - 1, n_cols), lax.rem(c + 1, n_cols)

    def along_rows(k):
        other = lax.rem(a + k, SIDE)
        return other, (other * SIDE + m, c)

    def along_cols(k):
        other = lax.rem(c + k, SIDE)
        return other, (r, other)

    barrier = pltpu.get_barrier_semaphore()
    for place in (
        (north, c), (south, c), (north, west), (north, east), (south, west), (south, east),
    ):
        pl.semaphore_signal(barrier, inc=1, device_id=place, device_id_type=MESH)

    def greet(k, carry):
        for along in (along_cols, along_rows):
            pl.semaphore_signal(barrier, inc=1, device_id=along(k)[1], device_id_type=MESH)
        return carry

    lax.fori_loop(1, SIDE, greet, 0)

    def halo(i, src, dst, row, col):
        return pltpu.make_async_remote_copy(
            src_ref=src,
            dst_ref=dst,
            send_sem=halo_send.at[i],
            recv_sem=halo_recv.at[i],
            device_id=(row, col),
            device_id_type=MESH,
        )

    halos = [
        halo(0, xb.at[:, ROWS - 1], halo_rows.at[0], south, c),
        halo(1, xb.at[:, 0], halo_rows.at[1], north, c),
        halo(2, edge.at[0], halo_edge.at[0], r, west),
        halo(3, edge.at[1], halo_edge.at[1], r, east),
        halo(4, edge.at[5], halo_edge.at[2], south, east),
        halo(5, edge.at[4], halo_edge.at[3], south, west),
        halo(6, edge.at[3], halo_edge.at[4], north, east),
        halo(7, edge.at[2], halo_edge.at[5], north, west),
    ]
    def block(k):
        return pl.ds(pl.multiple_of(k * PIECE, PIECE), PIECE)

    def exchange(stage, p, src, dst, along, mine):
        def send(k, carry):
            other, place = along(k)
            pltpu.make_async_remote_copy(
                src_ref=src.at[p, block(other)],
                dst_ref=dst.at[p, block(mine)],
                send_sem=sent.at[stage, p],
                recv_sem=received.at[stage, p],
                device_id=place,
                device_id_type=MESH,
            ).start()
            return carry

        lax.fori_loop(1, SIDE, send, 0)
        dst[p, block(mine)] = src[p, block(mine)]

    def wait_all(ref, p, sem):
        others = ref.at[p, pl.ds(0, PART - PIECE)]
        pltpu.make_async_copy(others, others, sem).wait()

    def expand_tile(f):
        def norm_rows(i, carry):
            v = xb[f, pl.ds(2 * i, 2)].astype(F32).reshape(64, WIDTH)
            normed[pl.ds(pl.multiple_of(i * 64, 64), 64)] = layer_norm(v, premix).astype(BF16)
            return carry

        lax.fori_loop(0, 4, norm_rows, 0)

        def expand(i, carry):
            lanes = pl.ds(pl.multiple_of(i * 256, 256), 256)
            g = gelu(matmul(normed[0:CELLS], we[:, lanes])).astype(BF16).astype(F32)
            ex[f, 1 : ROWS + 1, 0:COLS, lanes] = g.reshape(ROWS, COLS, 256)
            return carry

        lax.fori_loop(0, INNER // 256, expand, 0)

    for f in range(FORECASTS):
        ex[f, :, COLS:PADDED] = jnp.zeros((ROWS + 2, PADDED - COLS, INNER), F32)
    for i in range(2):
        place, cell = iota((PART, CELLS), 0), iota((PART, CELLS), 1)
        choose[i] = one_hot(cell == cells_of(i == 0, place))
        place, cell = iota((CELLS, PART), 1), iota((CELLS, PART), 0)
        restore[i] = one_hot(cell == cells_of(i == 0, place))
    loads[0].wait()
    loads[1].wait()
    premix = premix_ref[...]
    loads[2].wait()
    for load in loads[3:10]:
        load.start()
    expand_tile(0)

    loads[10].wait()
    place = iota((96, 512), 0)
    piece, index = place // 16, place % 16
    cell_f = jnp.where(piece < 2, index // 8, index % 2)
    cell_y = jnp.where(piece < 2, index % 8, jnp.where(piece < 4, 0, 7))
    cell_x = jnp.where(piece % 2 == 0, 0, 31)
    chosen = iota((96, 512), 1) == cell_f * CELLS + cell_y * COLS + cell_x
    edge[...] = matmul(one_hot(chosen), xb[...].reshape(512, WIDTH)).astype(BF16).reshape(6, 16, WIDTH)

    pl.semaphore_wait(barrier, 2 * (SIDE - 1) + 6)
    for copy in halos:
        copy.start()
    for load in loads[3:7]:
        load.wait()
    gain = gain_ref[...]

    def expand_halo(f):
        top = halo_rows[0, f].astype(F32) * jnp.where(r == 0, 0.0, 1.0)
        bottom = halo_rows[1, f].astype(F32) * jnp.where(r == n_rows - 1, 0.0, 1.0)
        normed[0:32] = layer_norm(top, premix).astype(BF16)
        normed[32:64] = layer_norm(bottom, premix).astype(BF16)
        place = iota((80, 96), 0)
        y, slot = place // 8, place % 8
        inside = ((y > 0) | (r > 0)) & ((y < 9) | (r < n_rows - 1))
        in_east = (slot == 0) & (c < n_cols - 1)
        in_west = (slot == 7) & (c > 0)
        source_east = jnp.where(y == 0, 48 + f, jnp.where(y == 9, 80 + f, f * 8 + y - 1))
        source_west = jnp.where(y == 0, 32 + f, jnp.where(y == 9, 64 + f, 16 + f * 8 + y - 1))
        source = jnp.where(in_east, source_east, source_west)
        chosen = (iota((80, 96), 1) == source) & inside & (in_east | in_west)
        sides = matmul(one_hot(chosen), halo_edge[...].reshape(96, WIDTH))
        normed[64:144] = layer_norm(sides, premix).astype(BF16)

        def expand(i, carry):
            lanes = pl.ds(pl.multiple_of(i * 256, 256), 256)
            g = gelu(matmul(normed[0:144], we[:, lanes])).astype(BF16).astype(F32)
            ex[f, 0, 0:COLS, lanes] = g[0:32]
            ex[f, ROWS + 1, 0:COLS, lanes] = g[32:64]
            ex[f, :, COLS:PADDED, lanes] = g[64:144].reshape(ROWS + 2, 8, 256)
            return carry

        lax.fori_loop(0, INNER // 256, expand, 0)

    def filter_row(f, y):
        for i in range(INNER // 256):
            lanes = slice(i * 256, (i + 1) * 256)
            around = [ex[f, y + q, :, lanes] for q in range(3)]
            taps = [
                sum(around[q] * dw_ref[q, s : s + 1, lanes] for q in range(3)) for s in range(3)
            ]
            total = pltpu.roll(taps[0], 1, 0) + taps[1] + pltpu.roll(taps[2], PADDED - 1, 0)
            act[pl.ds(pl.multiple_of(y * COLS, COLS), COLS), lanes] = gelu(
                total[0:COLS] + db_ref[:, lanes]
            ).astype(BF16)

    def convolve(f, inner, p):
        first, last = (1, 1 + INNER_ROWS) if inner else (0, ROWS)

        def filter_rows(y, carry):
            filter_row(f, y)
            return carry

        lax.fori_loop(first, last, filter_rows, 0)
        cells = slice(first * COLS, last * COLS)
        kind = 0 if inner else 1
        for i in range(2):
            lanes = slice(i * 512, (i + 1) * 512)
            chosen_act[:, lanes] = matmul(choose[kind, :, cells], act[cells, lanes]).astype(BF16)
        for i in range(2):
            lanes = slice(i * 256, (i + 1) * 256)
            residual = matmul(choose[kind], xb[f, :, :, lanes].reshape(CELLS, 256))
            conv[p, :, lanes] = (residual + matmul(chosen_act[...], wp[:, lanes])).astype(BF16)
        for i in range(2):
            rows = slice(i * 64, (i + 1) * 64)
            att[p, rows] = layer_norm(conv[p, rows].astype(F32), gain).astype(BF16)
        exchange(0, p, att, mid, along_rows, a)

    def convolve_inner(f, carry):
        @pl.when(f > 0)
        def _():
            expand_tile(f)

        convolve(f, True, f)
        return carry

    lax.fori_loop(0, FORECASTS, convolve_inner, 0)

    for copy in halos:
        copy.wait_recv()

    def convolve_outer(f, carry):
        expand_halo(f)
        convolve(f, False, FORECASTS + f)
        return carry

    lax.fori_loop(0, FORECASTS, convolve_outer, 0)

    row, col = iota((PART, PART), 0), iota((PART, PART), 1)
    swapped = row // 16 * 2 + row % 16 // 2 * 16 + row % 2
    orders[0] = one_hot(col == swapped)
    grouped = row % 8 * 16 + row % 64 // 8 * 2 + row // 64
    orders[1] = one_hot(col == grouped)
    ungrouped = row % 2 * 64 + row % 16 // 2 * 8 + row // 16
    orders[2] = one_hot(col == ungrouped)

    def reorder(i, v):
        return matmul(orders[i], v).astype(BF16)

    def pass_on(p):
        wait_all(mid, p, received.at[0, p])
        mid_out[p] = reorder(0, mid[p])
        exchange(1, p, mid_out, owned, along_cols, c)

    pass_on(0)

    loads[7].wait()
    flat[...] = jnp.zeros_like(flat)
    total = jnp.zeros((16, 256), F32)
    for q in range(15):
        flat[:, 0:15] = table_ref[q]
        total = total + (pltpu.roll(flat[...], 16 * q, 1) if q else flat[...])
    flat[...] = total

    def shift(h, carry):
        row = jnp.broadcast_to(flat[pl.ds(h, 1), :], (8, 256))
        for i in range(SIDE):
            moved = pltpu.roll(row, 137 + 16 * i, 1, stride=1, stride_axis=0)
            shifted[h, i * 8 : (i + 1) * 8] = moved[:, 0:128]
        return carry

    lax.fori_loop(0, 16, shift, 0)
    source, target = iota((512, 256), 0), iota((512, 256), 1)
    member = target % 64
    spread = one_hot(source == (target // 64) * 128 + 16 * (member // 8) + member % 8)

    def set_bias(q, carry):
        rest = jnp.concatenate([shifted[q * 4 + h] for h in range(4)], axis=1)
        parts = []
        for _ in range(3):
            parts.append(rest.astype(BF16))
            rest = rest - parts[-1].astype(F32)
        total = matmul(jnp.concatenate(parts, axis=0), spread)
        bias[q] = (total[0:64] + total[64:128] + total[128:192]) * LOG2E
        return carry

    lax.fori_loop(0, QUADS, set_bias, 0)
    loads[8].wait()

    head = iota((1, 128), 1) // 32
    own_lanes = [head == h for h in range(4)]

    def attend(p):
        wait_all(owned, p, received.at[1, p])
        xg[...] = reorder(1, owned[p])

        def project(i, carry):
            lanes = pl.ds(pl.multiple_of(i * 256, 256), 256)
            qkv[:, lanes] = matmul(xg[...], wqkv[:, lanes]).astype(BF16)
            return carry

        lax.fori_loop(0, 6, project, 0)

        for t in range(GROUPS):
            rows = slice(t * 64, (t + 1) * 64)
            for q in range(QUADS):
                lanes = slice(q * 128, (q + 1) * 128)
                query = qkv[rows, lanes]
                keys = qkv[rows, 512 + q * 128 : 640 + q * 128]
                values = qkv[rows, 1024 + q * 128 : 1152 + q * 128]
                apart = jnp.concatenate([query * one_hot(own_lanes[h]) for h in range(4)], axis=0)
                scores = lax.dot_general(
                    keys, apart, (((1,), (1,)), ((), ())), preferred_element_type=F32
                )
                scores = scores * (32**-0.5 * LOG2E) + bias[q]
                powers = jnp.exp2(scores - jnp.max(scores, axis=0, keepdims=True))
                share = 1.0 / jnp.sum(powers, axis=0, keepdims=True)
                attention = (powers * share).astype(BF16)
                mixed = lax.dot_general(
                    attention, values, (((0,), (0,)), ((), ())), preferred_element_type=F32
                )
                total = jnp.where(own_lanes[0], mixed[0:64], 0.0)
                for h in range(1, 4):
                    total = jnp.where(own_lanes[h], mixed[h * 64 : (h + 1) * 64], total)
                context[rows, lanes] = total.astype(BF16)

        answers[p] = reorder(2, context[...])
        exchange(2, p, answers, mid_back, along_cols, c)

    def pass_back(p):
        wait_all(mid_back, p, received.at[2, p])
        mid_return[p] = reorder(0, mid_back[p])
        exchange(3, p, mid_return, returned, along_rows, a)

    def step(i, carry):
        @pl.when(i < PARTS)
        def _():
            pass_on(i)

        @pl.when(i <= PARTS)
        def _():
            attend(i - 1)

        @pl.when(i >= 2)
        def _():
            pass_back(i - 2)

        return carry

    lax.fori_loop(1, PARTS + 2, step, 0)
    loads[9].wait()

    def finish(p, carry):
        wait_all(returned, p, received.at[3, p])
        f, kind = p % FORECASTS, p // FORECASTS
        for i in range(2):
            lanes = slice(i * 256, (i + 1) * 256)
            total = conv[p, :, lanes].astype(F32) + matmul(returned[p], wo[:, lanes])
            placed = matmul(restore[kind], total.astype(BF16))

            @pl.when(kind == 0)
            def _():
                finished[f, :, lanes] = placed

            @pl.when(kind == 1)
            def _():
                out_ref[f, :, :, lanes] = (
                    (finished[f, :, lanes] + placed).astype(BF16).reshape(ROWS, COLS, 256)
                )

        return carry

    lax.fori_loop(0, PARTS, finish, 0)

    for copy in halos:
        copy.wait_send()

    def drain(p, carry):
        for stage, ref in enumerate((att, mid_out, answers, mid_return)):
            wait_all(ref, p, sent.at[stage, p])
        return carry

    lax.fori_loop(0, PARTS, drain, 0)


def on_device(
    atmosphere_variables,
    premix_gain_vector,
    expand_weight,
    depth_weight,
    depth_bias,
    project_weight,
    norm_attn,
    qkv_weight,
    out_weight,
    bias_table,
):
    whole = pl.BlockSpec(memory_space=pltpu.HBM)
    tile = (FORECASTS, ROWS, COLS, WIDTH)
    parts = pltpu.VMEM((PARTS, PART, WIDTH), BF16)
    return pl.pallas_call(
        kernel,
        out_shape=pltpu.VMEM(tile, BF16),
        in_specs=[whole] * 10,
        out_specs=pl.BlockSpec(memory_space=pltpu.VMEM),
        scratch_shapes=[
            pltpu.VMEM(tile, BF16),
            pltpu.VMEM((1, WIDTH), F32),
            pltpu.VMEM((WIDTH, INNER), BF16),
            pltpu.VMEM((3, 3, INNER), F32),
            pltpu.VMEM((1, INNER), F32),
            pltpu.VMEM((INNER, WIDTH), BF16),
            pltpu.VMEM((1, WIDTH), F32),
            pltpu.VMEM((WIDTH, 3 * WIDTH), BF16),
            pltpu.VMEM((WIDTH, WIDTH), BF16),
            pltpu.VMEM((15, 16, 15), F32),
            pltpu.VMEM((6, 16, WIDTH), BF16),
            pltpu.VMEM((2, FORECASTS, COLS, WIDTH), BF16),
            pltpu.VMEM((6, 16, WIDTH), BF16),
            pltpu.VMEM((CELLS, WIDTH), BF16),
            pltpu.VMEM((FORECASTS, ROWS + 2, PADDED, INNER), F32),
            pltpu.VMEM((CELLS, INNER), BF16),
            pltpu.VMEM((PART, INNER), BF16),
            parts,
            pltpu.VMEM((2, PART, CELLS), BF16),
            pltpu.VMEM((2, CELLS, PART), BF16),
            pltpu.VMEM((FORECASTS, CELLS, WIDTH), F32),
            *[parts] * 8,
            pltpu.VMEM((3, PART, PART), BF16),
            pltpu.VMEM((PART, WIDTH), BF16),
            pltpu.VMEM((PART, 3 * WIDTH), BF16),
            pltpu.VMEM((PART, WIDTH), BF16),
            pltpu.VMEM((16, 256), F32),
            pltpu.VMEM((16, MEMBERS, 128), F32),
            pltpu.VMEM((QUADS, MEMBERS, 256), F32),
            pltpu.SemaphoreType.DMA((11,)),
            pltpu.SemaphoreType.DMA((8,)),
            pltpu.SemaphoreType.DMA((8,)),
            pltpu.SemaphoreType.DMA((4, PARTS)),
            pltpu.SemaphoreType.DMA((4, PARTS)),
        ],
        compiler_params=pltpu.CompilerParams(
            collective_id=0, has_side_effects=True, vmem_limit_bytes=56 * 1024 * 1024
        ),
        name="maxvit_layer",
    )(
        atmosphere_variables,
        premix_gain_vector.reshape(1, WIDTH),
        expand_weight,
        depth_weight,
        depth_bias.reshape(1, INNER),
        project_weight,
        norm_attn.reshape(1, WIDTH),
        qkv_weight,
        out_weight,
        bias_table.transpose(1, 0, 2),
    )


def solution(mesh):
    return jax.shard_map(
        on_device,
        mesh=mesh,
        in_specs=(P(None, "rows", "cols", None), P(), P(), P(), P(), P(), P(), P(), P(), P()),
        out_specs=P(None, "rows", "cols", None),
        check_vma=False,
    )
```

```python
import jax
import jax.numpy as jnp
from jax import lax
from jax.experimental import pallas as pl
from jax.experimental.pallas import tpu as pltpu
from jax.sharding import PartitionSpec as P

MESH = pl.DeviceIdType.MESH
F32 = jnp.float32
BF16 = jnp.bfloat16

FORECASTS = 2
ROWS = 8
COLS = 32
CELLS = ROWS * COLS
WIDTH = 512
INNER = 1024
SIDE = 8
PARTS = 4
PART = FORECASTS * CELLS // PARTS
INNER_ROWS = 5
PIECE = PART // SIDE
GROUPS = PIECE // SIDE
MEMBERS = SIDE * SIDE
PADDED = 40
QUADS = 4
LOG2E = 1.4426950408889634


def gelu(v):
    half = 0.5 * v
    return half + half * jnp.tanh(v * (0.7978845608028654 + 0.035677408136300125 * (v * v)))


def layer_norm(v, gain):
    centred = v - jnp.mean(v, axis=-1, keepdims=True)
    variance = jnp.mean(centred * centred, axis=-1, keepdims=True)
    return centred * lax.rsqrt(variance + 1e-05) * gain


def iota(shape, dim):
    return lax.broadcasted_iota(jnp.int32, shape, dim)


def one_hot(condition):
    return jnp.where(condition, 1.0, 0.0).astype(BF16)


def place_of(inner, cell):
    y, x = cell >> 5, cell & 31
    if inner:
        k = (y - 1) * 30 + x - 1
        return jnp.where((y > 0) & (y < 6) & (x > 0) & (x < 31) & (k < PART), k, -1)
    sides = jnp.where(x == 0, 2 * y + 30, jnp.where(x == 31, 2 * y + 31, -1))
    fifth = jnp.where(x == 0, 40, jnp.where(x > 8, 32 + x, -1))
    return jnp.where(
        y == 0, x, jnp.where(y < 5, sides, jnp.where(y == 5, fifth, cell - (CELLS - PART)))
    )


def matmul(a, b):
    return jnp.dot(a, b, preferred_element_type=F32)


def kernel(
    x_hbm, premix_hbm, we_hbm, dw_hbm, db_hbm, wp_hbm, gain_hbm, wqkv_hbm, wo_hbm, table_hbm,
    out_ref,
    xb, premix_ref, we, dw_ref, db_ref, wp, gain_ref, wqkv, wo, table_ref,
    edge, halo_rows, halo_edge, normed, ex, act, chosen_act, conv, choose, restore, finished,
    att, mid, mid_out, owned, answers, mid_back, mid_return, returned,
    orders, xg, qkv, context, flat, shifted, bias,
    load_sem, halo_send, halo_recv, sent, received,
):
    r = lax.axis_index("rows")
    c = lax.axis_index("cols")
    n_rows = lax.axis_size("rows")
    n_cols = lax.axis_size("cols")
    a, m = r // SIDE, r % SIDE

    loads = [
        pltpu.make_async_copy(src, dst, load_sem.at[i])
        for i, (src, dst) in enumerate(
            (
                (x_hbm.at[0], xb.at[0]), (premix_hbm, premix_ref), (we_hbm, we), (dw_hbm, dw_ref),
                (db_hbm, db_ref), (wp_hbm, wp), (gain_hbm, gain_ref), (table_hbm, table_ref),
                (wqkv_hbm, wqkv), (wo_hbm, wo), (x_hbm.at[1], xb.at[1]),
            )
        )
    ]
    for load in loads[:3] + loads[10:]:
        load.start()

    north, south = lax.rem(r + n_rows - 1, n_rows), lax.rem(r + 1, n_rows)
    west, east = lax.rem(c + n_cols - 1, n_cols), lax.rem(c + 1, n_cols)

    def along_rows(k):
        other = lax.rem(a + k, SIDE)
        return other, (other * SIDE + m, c)

    def along_cols(k):
        other = lax.rem(c + k, SIDE)
        return other, (r, other)

    barrier = pltpu.get_barrier_semaphore()
    for place in (
        (north, c), (south, c), (north, west), (north, east), (south, west), (south, east),
    ):
        pl.semaphore_signal(barrier, inc=1, device_id=place, device_id_type=MESH)

    def greet(k, carry):
        for along in (along_cols, along_rows):
            pl.semaphore_signal(barrier, inc=1, device_id=along(k)[1], device_id_type=MESH)
        return carry

    lax.fori_loop(1, SIDE, greet, 0)

    def halo(i, src, dst, row, col):
        return pltpu.make_async_remote_copy(
            src_ref=src,
            dst_ref=dst,
            send_sem=halo_send.at[i],
            recv_sem=halo_recv.at[i],
            device_id=(row, col),
            device_id_type=MESH,
        )

    halos = [
        halo(0, xb.at[:, ROWS - 1], halo_rows.at[0], south, c),
        halo(1, xb.at[:, 0], halo_rows.at[1], north, c),
        halo(2, edge.at[0], halo_edge.at[0], r, west),
        halo(3, edge.at[1], halo_edge.at[1], r, east),
        halo(4, edge.at[5], halo_edge.at[2], south, east),
        halo(5, edge.at[4], halo_edge.at[3], south, west),
        halo(6, edge.at[3], halo_edge.at[4], north, east),
        halo(7, edge.at[2], halo_edge.at[5], north, west),
    ]
    def block(k):
        return pl.ds(pl.multiple_of(k * PIECE, PIECE), PIECE)

    def exchange(stage, p, src, dst, along, mine):
        def send(k, carry):
            other, place = along(k)
            pltpu.make_async_remote_copy(
                src_ref=src.at[p, block(other)],
                dst_ref=dst.at[p, block(mine)],
                send_sem=sent.at[stage, p],
                recv_sem=received.at[stage, p],
                device_id=place,
                device_id_type=MESH,
            ).start()
            return carry

        lax.fori_loop(1, SIDE, send, 0)
        dst[p, block(mine)] = src[p, block(mine)]

    def wait_all(ref, p, sem):
        others = ref.at[p, pl.ds(0, PART - PIECE)]
        pltpu.make_async_copy(others, others, sem).wait()

    def expand_tile(f):
        def norm_rows(i, carry):
            v = xb[f, pl.ds(2 * i, 2)].astype(F32).reshape(64, WIDTH)
            normed[pl.ds(pl.multiple_of(i * 64, 64), 64)] = layer_norm(v, premix).astype(BF16)
            return carry

        lax.fori_loop(0, 4, norm_rows, 0, unroll=True)

        def expand(i, carry):
            lanes = pl.ds(pl.multiple_of(i * 256, 256), 256)
            g = gelu(matmul(normed[0:CELLS], we[:, lanes])).astype(BF16).astype(F32)
            ex[f, 1 : ROWS + 1, 0:COLS, lanes] = g.reshape(ROWS, COLS, 256)
            return carry

        lax.fori_loop(0, INNER // 256, expand, 0, unroll=True)

    for f in range(FORECASTS):
        ex[f, :, COLS:PADDED] = jnp.zeros((ROWS + 2, PADDED - COLS, INNER), F32)
    for i in range(2):
        choose[i] = one_hot(iota((PART, CELLS), 0) == place_of(i == 0, iota((1, CELLS), 1)))
    loads[0].wait()
    loads[1].wait()
    premix = premix_ref[...]
    loads[2].wait()
    for load in loads[3:10]:
        load.start()
    expand_tile(0)

    loads[10].wait()
    place = iota((96, 1), 0)
    piece, index = place >> 4, place & 15
    cell_f = jnp.where(piece < 2, index >> 3, index & 1)
    cell_y = jnp.where(piece < 2, index & 7, jnp.where(piece < 4, 0, 7))
    cell_x = (piece & 1) * 31
    chosen = iota((96, 512), 1) == cell_f * CELLS + cell_y * COLS + cell_x
    edge[...] = matmul(one_hot(chosen), xb[...].reshape(512, WIDTH)).astype(BF16).reshape(6, 16, WIDTH)

    pl.semaphore_wait(barrier, 2 * (SIDE - 1) + 6)
    for copy in halos:
        copy.start()
    for load in loads[3:7]:
        load.wait()
    gain = gain_ref[...]

    def expand_halo(f):
        top = halo_rows[0, f].astype(F32) * jnp.where(r == 0, 0.0, 1.0)
        bottom = halo_rows[1, f].astype(F32) * jnp.where(r == n_rows - 1, 0.0, 1.0)
        normed[0:32] = layer_norm(top, premix).astype(BF16)
        normed[32:64] = layer_norm(bottom, premix).astype(BF16)
        place = iota((80, 1), 0)
        y, slot = place >> 3, place & 7
        inside = ((y > 0) | (r > 0)) & ((y < 9) | (r < n_rows - 1))
        in_east = (slot == 0) & (c < n_cols - 1)
        in_west = (slot == 7) & (c > 0)
        source_east = jnp.where(y == 0, 48 + f, jnp.where(y == 9, 80 + f, f * 8 + y - 1))
        source_west = jnp.where(y == 0, 32 + f, jnp.where(y == 9, 64 + f, 16 + f * 8 + y - 1))
        source = jnp.where(in_east, source_east, source_west)
        source = jnp.where(inside & (in_east | in_west), source, -1)
        chosen = iota((80, 96), 1) == source
        sides = matmul(one_hot(chosen), halo_edge[...].reshape(96, WIDTH))
        normed[64:144] = layer_norm(sides, premix).astype(BF16)

        def expand(i, carry):
            lanes = pl.ds(pl.multiple_of(i * 256, 256), 256)
            g = gelu(matmul(normed[0:144], we[:, lanes])).astype(BF16).astype(F32)
            ex[f, 0, 0:COLS, lanes] = g[0:32]
            ex[f, ROWS + 1, 0:COLS, lanes] = g[32:64]
            ex[f, :, COLS:PADDED, lanes] = g[64:144].reshape(ROWS + 2, 8, 256)
            return carry

        lax.fori_loop(0, INNER // 256, expand, 0, unroll=True)

    def filter_row(f, y):
        for i in range(INNER // 256):
            lanes = slice(i * 256, (i + 1) * 256)
            around = [ex[f, y + q, :, lanes] for q in range(3)]
            taps = [
                sum(around[q] * dw_ref[q, s : s + 1, lanes] for q in range(3)) for s in range(3)
            ]
            total = pltpu.roll(taps[0], 1, 0) + taps[1] + pltpu.roll(taps[2], PADDED - 1, 0)
            act[pl.ds(pl.multiple_of(y * COLS, COLS), COLS), lanes] = gelu(
                total[0:COLS] + db_ref[:, lanes]
            ).astype(BF16)

    def convolve(f, inner, p):
        first, last = (1, 1 + INNER_ROWS) if inner else (0, ROWS)

        def filter_rows(y, carry):
            filter_row(f, y)
            return carry

        lax.fori_loop(first, last, filter_rows, 0)
        cells = slice(first * COLS, last * COLS)
        kind = 0 if inner else 1
        for i in range(2):
            lanes = slice(i * 512, (i + 1) * 512)
            chosen_act[:, lanes] = matmul(choose[kind, :, cells], act[cells, lanes]).astype(BF16)
        for i in range(2):
            lanes = slice(i * 256, (i + 1) * 256)
            residual = matmul(choose[kind], xb[f, :, :, lanes].reshape(CELLS, 256))
            conv[p, :, lanes] = (residual + matmul(chosen_act[...], wp[:, lanes])).astype(BF16)
        for i in range(2):
            rows = slice(i * 64, (i + 1) * 64)
            att[p, rows] = layer_norm(conv[p, rows].astype(F32), gain).astype(BF16)
        exchange(0, p, att, mid, along_rows, a)

    def convolve_inner(f, carry):
        @pl.when(f > 0)
        def _():
            expand_tile(f)

        convolve(f, True, f)
        return carry

    lax.fori_loop(0, FORECASTS, convolve_inner, 0)

    for copy in halos:
        copy.wait_recv()

    def convolve_outer(f, carry):
        expand_halo(f)
        convolve(f, False, FORECASTS + f)
        return carry

    lax.fori_loop(0, FORECASTS, convolve_outer, 0)

    row, col = iota((PART, 1), 0), iota((PART, PART), 1)
    orders[0] = one_hot(col == ((row >> 4) << 1) + (((row & 15) >> 1) << 4) + (row & 1))
    orders[1] = one_hot(col == ((row & 7) << 4) + (((row & 63) >> 3) << 1) + (row >> 6))
    orders[2] = one_hot(col == ((row & 1) << 6) + (((row & 15) >> 1) << 3) + (row >> 4))

    def reorder(i, v):
        return matmul(orders[i], v).astype(BF16)

    def pass_on(p):
        wait_all(mid, p, received.at[0, p])
        mid_out[p] = reorder(0, mid[p])
        exchange(1, p, mid_out, owned, along_cols, c)

    pass_on(0)

    loads[7].wait()
    flat[...] = jnp.zeros_like(flat)
    total = jnp.zeros((16, 256), F32)
    for q in range(15):
        flat[:, 0:15] = table_ref[q]
        total = total + (pltpu.roll(flat[...], 16 * q, 1) if q else flat[...])
    flat[...] = total

    def shift(h, carry):
        row = jnp.broadcast_to(flat[pl.ds(h, 1), :], (8, 256))
        for i in range(SIDE):
            moved = pltpu.roll(row, 137 + 16 * i, 1, stride=1, stride_axis=0)
            shifted[h, i * 8 : (i + 1) * 8] = moved[:, 0:128]
        return carry

    lax.fori_loop(0, 16, shift, 0, unroll=True)
    target = iota((1, 256), 1)
    lane = ((target >> 6) << 7) + (((target & 63) >> 3) << 4) + (target & 7)
    spread = one_hot(iota((512, 256), 0) == lane)

    def set_bias(q, carry):
        rest = jnp.concatenate([shifted[q * 4 + h] for h in range(4)], axis=1)
        parts = []
        for _ in range(3):
            parts.append(rest.astype(BF16))
            rest = rest - parts[-1].astype(F32)
        total = matmul(jnp.concatenate(parts, axis=0), spread)
        bias[q] = (total[0:64] + total[64:128] + total[128:192]) * LOG2E
        return carry

    lax.fori_loop(0, QUADS, set_bias, 0)
    loads[8].wait()

    head = iota((1, 128), 1) >> 5
    own_lanes = [head == h for h in range(4)]

    def attend(p):
        wait_all(owned, p, received.at[1, p])
        xg[...] = reorder(1, owned[p])

        def project(i, carry):
            lanes = pl.ds(pl.multiple_of(i * 256, 256), 256)
            qkv[:, lanes] = matmul(xg[...], wqkv[:, lanes]).astype(BF16)
            return carry

        lax.fori_loop(0, 6, project, 0, unroll=True)

        for t in range(GROUPS):
            rows = slice(t * 64, (t + 1) * 64)
            for q in range(QUADS):
                lanes = slice(q * 128, (q + 1) * 128)
                query = qkv[rows, lanes]
                keys = qkv[rows, 512 + q * 128 : 640 + q * 128]
                values = qkv[rows, 1024 + q * 128 : 1152 + q * 128]
                apart = jnp.concatenate([query * one_hot(own_lanes[h]) for h in range(4)], axis=0)
                scores = lax.dot_general(
                    keys, apart, (((1,), (1,)), ((), ())), preferred_element_type=F32
                )
                scores = scores * (32**-0.5 * LOG2E) + bias[q]
                powers = jnp.exp2(scores - jnp.max(scores, axis=0, keepdims=True))
                share = 1.0 / jnp.sum(powers, axis=0, keepdims=True)
                attention = (powers * share).astype(BF16)
                mixed = lax.dot_general(
                    attention, values, (((0,), (0,)), ((), ())), preferred_element_type=F32
                )
                total = jnp.where(own_lanes[0], mixed[0:64], 0.0)
                for h in range(1, 4):
                    total = jnp.where(own_lanes[h], mixed[h * 64 : (h + 1) * 64], total)
                context[rows, lanes] = total.astype(BF16)

        answers[p] = reorder(2, context[...])
        exchange(2, p, answers, mid_back, along_cols, c)

    def pass_back(p):
        wait_all(mid_back, p, received.at[2, p])
        mid_return[p] = reorder(0, mid_back[p])

        def send(k, carry):
            @pl.when(k != a)
            def _():
                pltpu.make_async_remote_copy(
                    src_ref=mid_return.at[p, block(k)],
                    dst_ref=returned.at[p, block(a)],
                    send_sem=sent.at[3, p],
                    recv_sem=received.at[3, p],
                    device_id=(k * SIDE + m, c),
                    device_id_type=MESH,
                ).start()

            return carry

        lax.fori_loop(0, SIDE, send, 0)
        returned[p, block(a)] = mid_return[p, block(a)]

    def step(i, carry):
        @pl.when(i < PARTS)
        def _():
            pass_on(i)

        @pl.when(i <= PARTS)
        def _():
            attend(i - 1)

        @pl.when(i >= 2)
        def _():
            pass_back(i - 2)

        return carry

    lax.fori_loop(1, PARTS + 2, step, 0)
    loads[9].wait()
    for i in range(2):
        restore[i] = one_hot(iota((CELLS, PART), 1) == place_of(i == 0, iota((CELLS, 1), 0)))

    def finish(p, carry):
        wait_all(returned, p, received.at[3, p])
        f, kind = p % FORECASTS, p // FORECASTS
        for i in range(2):
            lanes = slice(i * 256, (i + 1) * 256)
            total = conv[p, :, lanes].astype(F32) + matmul(returned[p], wo[:, lanes])
            placed = matmul(restore[kind], total.astype(BF16))

            @pl.when(kind == 0)
            def _():
                finished[f, :, lanes] = placed

            @pl.when(kind == 1)
            def _():
                out_ref[f, :, :, lanes] = (
                    (finished[f, :, lanes] + placed).astype(BF16).reshape(ROWS, COLS, 256)
                )

        return carry

    lax.fori_loop(0, PARTS, finish, 0)

    for copy in halos:
        copy.wait_send()

    def drain(p, carry):
        for stage, ref in enumerate((att, mid_out, answers, mid_return)):
            wait_all(ref, p, sent.at[stage, p])
        return carry

    lax.fori_loop(0, PARTS, drain, 0)


def on_device(
    atmosphere_variables,
    premix_gain_vector,
    expand_weight,
    depth_weight,
    depth_bias,
    project_weight,
    norm_attn,
    qkv_weight,
    out_weight,
    bias_table,
):
    whole = pl.BlockSpec(memory_space=pltpu.HBM)
    tile = (FORECASTS, ROWS, COLS, WIDTH)
    parts = pltpu.VMEM((PARTS, PART, WIDTH), BF16)
    return pl.pallas_call(
        kernel,
        out_shape=pltpu.VMEM(tile, BF16),
        in_specs=[whole] * 10,
        out_specs=pl.BlockSpec(memory_space=pltpu.VMEM),
        scratch_shapes=[
            pltpu.VMEM(tile, BF16),
            pltpu.VMEM((1, WIDTH), F32),
            pltpu.VMEM((WIDTH, INNER), BF16),
            pltpu.VMEM((3, 3, INNER), F32),
            pltpu.VMEM((1, INNER), F32),
            pltpu.VMEM((INNER, WIDTH), BF16),
            pltpu.VMEM((1, WIDTH), F32),
            pltpu.VMEM((WIDTH, 3 * WIDTH), BF16),
            pltpu.VMEM((WIDTH, WIDTH), BF16),
            pltpu.VMEM((15, 16, 15), F32),
            pltpu.VMEM((6, 16, WIDTH), BF16),
            pltpu.VMEM((2, FORECASTS, COLS, WIDTH), BF16),
            pltpu.VMEM((6, 16, WIDTH), BF16),
            pltpu.VMEM((CELLS, WIDTH), BF16),
            pltpu.VMEM((FORECASTS, ROWS + 2, PADDED, INNER), F32),
            pltpu.VMEM((CELLS, INNER), BF16),
            pltpu.VMEM((PART, INNER), BF16),
            parts,
            pltpu.VMEM((2, PART, CELLS), BF16),
            pltpu.VMEM((2, CELLS, PART), BF16),
            pltpu.VMEM((FORECASTS, CELLS, WIDTH), F32),
            *[parts] * 8,
            pltpu.VMEM((3, PART, PART), BF16),
            pltpu.VMEM((PART, WIDTH), BF16),
            pltpu.VMEM((PART, 3 * WIDTH), BF16),
            pltpu.VMEM((PART, WIDTH), BF16),
            pltpu.VMEM((16, 256), F32),
            pltpu.VMEM((16, MEMBERS, 128), F32),
            pltpu.VMEM((QUADS, MEMBERS, 256), F32),
            pltpu.SemaphoreType.DMA((11,)),
            pltpu.SemaphoreType.DMA((8,)),
            pltpu.SemaphoreType.DMA((8,)),
            pltpu.SemaphoreType.DMA((4, PARTS)),
            pltpu.SemaphoreType.DMA((4, PARTS)),
        ],
        compiler_params=pltpu.CompilerParams(
            collective_id=0, has_side_effects=True, vmem_limit_bytes=56 * 1024 * 1024
        ),
        name="maxvit_layer",
    )(
        atmosphere_variables,
        premix_gain_vector.reshape(1, WIDTH),
        expand_weight,
        depth_weight,
        depth_bias.reshape(1, INNER),
        project_weight,
        norm_attn.reshape(1, WIDTH),
        qkv_weight,
        out_weight,
        bias_table.transpose(1, 0, 2),
    )


def solution(mesh):
    return jax.shard_map(
        on_device,
        mesh=mesh,
        in_specs=(P(None, "rows", "cols", None), P(), P(), P(), P(), P(), P(), P(), P(), P()),
        out_specs=P(None, "rows", "cols", None),
        check_vma=False,
    )
```

```python
import jax
import jax.numpy as jnp
from jax import lax
from jax.experimental import pallas as pl
from jax.experimental.pallas import tpu as pltpu
from jax.sharding import PartitionSpec as P

MESH = pl.DeviceIdType.MESH
F32 = jnp.float32
BF16 = jnp.bfloat16

FORECASTS = 2
ROWS = 8
COLS = 32
CELLS = ROWS * COLS
WIDTH = 512
INNER = 1024
SIDE = 8
PARTS = 4
PART = FORECASTS * CELLS // PARTS
INNER_ROWS = 5
PIECE = PART // SIDE
GROUPS = PIECE // SIDE
MEMBERS = SIDE * SIDE
PADDED = 40
QUADS = 4
LOG2E = 1.4426950408889634


def gelu(v):
    half = 0.5 * v
    return half + half * jnp.tanh(v * (0.7978845608028654 + 0.035677408136300125 * (v * v)))


def layer_norm(v, gain):
    centred = v - jnp.mean(v, axis=-1, keepdims=True)
    variance = jnp.mean(centred * centred, axis=-1, keepdims=True)
    return centred * lax.rsqrt(variance + 1e-05) * gain


def iota(shape, dim):
    return lax.broadcasted_iota(jnp.int32, shape, dim)


def one_hot(condition):
    return jnp.where(condition, 1.0, 0.0).astype(BF16)


def place_of(inner, cell):
    y, x = cell >> 5, cell & 31
    if inner:
        k = (y - 1) * 30 + x - 1
        return jnp.where((y > 0) & (y < 6) & (x > 0) & (x < 31) & (k < PART), k, -1)
    sides = jnp.where(x == 0, 2 * y + 30, jnp.where(x == 31, 2 * y + 31, -1))
    fifth = jnp.where(x == 0, 40, jnp.where(x > 8, 32 + x, -1))
    return jnp.where(
        y == 0, x, jnp.where(y < 5, sides, jnp.where(y == 5, fifth, cell - (CELLS - PART)))
    )


def matmul(a, b):
    return jnp.dot(a, b, preferred_element_type=F32)


def kernel(
    x_hbm, premix_hbm, we_hbm, dw_hbm, db_hbm, wp_hbm, gain_hbm, wqkv_hbm, wo_hbm, table_hbm,
    out_ref,
    xb, premix_ref, we, dw_ref, db_ref, wp, gain_ref, wqkv, wo, table_ref,
    edge, halo_rows, halo_edge, normed, ex, act, chosen_act, conv, choose, restore, finished,
    att, mid, mid_out, owned, answers, mid_back, mid_return, returned,
    orders, xg, qkv, context, flat, shifted, bias,
    load_sem, halo_send, halo_recv, sent, received,
):
    r = lax.axis_index("rows")
    c = lax.axis_index("cols")
    n_rows = lax.axis_size("rows")
    n_cols = lax.axis_size("cols")
    a, m = r // SIDE, r % SIDE

    loads = [
        pltpu.make_async_copy(src, dst, load_sem.at[i])
        for i, (src, dst) in enumerate(
            (
                (x_hbm.at[0], xb.at[0]), (premix_hbm, premix_ref), (we_hbm, we), (dw_hbm, dw_ref),
                (db_hbm, db_ref), (wp_hbm, wp), (gain_hbm, gain_ref), (table_hbm, table_ref),
                (wqkv_hbm, wqkv), (wo_hbm, wo), (x_hbm.at[1], xb.at[1]),
            )
        )
    ]
    for load in loads[:3]:
        load.start()

    north, south = lax.rem(r + n_rows - 1, n_rows), lax.rem(r + 1, n_rows)
    west, east = lax.rem(c + n_cols - 1, n_cols), lax.rem(c + 1, n_cols)

    def along_rows(k):
        other = lax.rem(a + k, SIDE)
        return other, (other * SIDE + m, c)

    def along_cols(k):
        other = lax.rem(c + k, SIDE)
        return other, (r, other)

    barrier = pltpu.get_barrier_semaphore()
    for place in (
        (north, c), (south, c), (north, west), (north, east), (south, west), (south, east),
    ):
        pl.semaphore_signal(barrier, inc=1, device_id=place, device_id_type=MESH)

    def greet(k, carry):
        for along in (along_cols, along_rows):
            pl.semaphore_signal(barrier, inc=1, device_id=along(k)[1], device_id_type=MESH)
        return carry

    lax.fori_loop(1, SIDE, greet, 0)

    def halo(i, src, dst, row, col):
        return pltpu.make_async_remote_copy(
            src_ref=src,
            dst_ref=dst,
            send_sem=halo_send.at[i],
            recv_sem=halo_recv.at[i],
            device_id=(row, col),
            device_id_type=MESH,
        )

    halos = [
        halo(0, xb.at[:, ROWS - 1], halo_rows.at[0], south, c),
        halo(1, xb.at[:, 0], halo_rows.at[1], north, c),
        halo(2, edge.at[0], halo_edge.at[0], r, west),
        halo(3, edge.at[1], halo_edge.at[1], r, east),
        halo(4, edge.at[5], halo_edge.at[2], south, east),
        halo(5, edge.at[4], halo_edge.at[3], south, west),
        halo(6, edge.at[3], halo_edge.at[4], north, east),
        halo(7, edge.at[2], halo_edge.at[5], north, west),
    ]
    def block(k):
        return pl.ds(pl.multiple_of(k * PIECE, PIECE), PIECE)

    def exchange(stage, p, src, dst, along, mine):
        def send(k, carry):
            other, place = along(k)
            pltpu.make_async_remote_copy(
                src_ref=src.at[p, block(other)],
                dst_ref=dst.at[p, block(mine)],
                send_sem=sent.at[stage, p],
                recv_sem=received.at[stage, p],
                device_id=place,
                device_id_type=MESH,
            ).start()
            return carry

        lax.fori_loop(1, SIDE, send, 0)
        dst[p, block(mine)] = src[p, block(mine)]

    def wait_all(ref, p, sem):
        others = ref.at[p, pl.ds(0, PART - PIECE)]
        pltpu.make_async_copy(others, others, sem).wait()

    def expand_tile(f):
        def norm_rows(i, carry):
            v = xb[f, pl.ds(2 * i, 2)].astype(F32).reshape(64, WIDTH)
            normed[pl.ds(pl.multiple_of(i * 64, 64), 64)] = layer_norm(v, premix).astype(BF16)
            return carry

        lax.fori_loop(0, 4, norm_rows, 0, unroll=True)

        def expand(i, carry):
            lanes = pl.ds(pl.multiple_of(i * 256, 256), 256)
            g = gelu(matmul(normed[0:CELLS], we[:, lanes])).astype(BF16).astype(F32)
            ex[f, 1 : ROWS + 1, 0:COLS, lanes] = g.reshape(ROWS, COLS, 256)
            return carry

        lax.fori_loop(0, INNER // 256, expand, 0, unroll=True)

    for f in range(FORECASTS):
        ex[f, :, COLS:PADDED] = jnp.zeros((ROWS + 2, PADDED - COLS, INNER), F32)
    for i in range(2):
        choose[i] = one_hot(iota((PART, CELLS), 0) == place_of(i == 0, iota((1, CELLS), 1)))
    loads[0].wait()
    for load in loads[3:]:
        load.start()
    loads[1].wait()
    premix = premix_ref[...]
    loads[2].wait()
    expand_tile(0)
    for load in loads[3:7]:
        load.wait()
    gain = gain_ref[...]

    def expand_halo(f):
        top = halo_rows[0, f].astype(F32) * jnp.where(r == 0, 0.0, 1.0)
        bottom = halo_rows[1, f].astype(F32) * jnp.where(r == n_rows - 1, 0.0, 1.0)
        normed[0:32] = layer_norm(top, premix).astype(BF16)
        normed[32:64] = layer_norm(bottom, premix).astype(BF16)
        place = iota((80, 1), 0)
        y, slot = place >> 3, place & 7
        inside = ((y > 0) | (r > 0)) & ((y < 9) | (r < n_rows - 1))
        in_east = (slot == 0) & (c < n_cols - 1)
        in_west = (slot == 7) & (c > 0)
        source_east = jnp.where(y == 0, 48 + f, jnp.where(y == 9, 80 + f, f * 8 + y - 1))
        source_west = jnp.where(y == 0, 32 + f, jnp.where(y == 9, 64 + f, 16 + f * 8 + y - 1))
        source = jnp.where(in_east, source_east, source_west)
        source = jnp.where(inside & (in_east | in_west), source, -1)
        chosen = iota((80, 96), 1) == source
        sides = matmul(one_hot(chosen), halo_edge[...].reshape(96, WIDTH))
        normed[64:144] = layer_norm(sides, premix).astype(BF16)

        def expand(i, carry):
            lanes = pl.ds(pl.multiple_of(i * 256, 256), 256)
            g = gelu(matmul(normed[0:144], we[:, lanes])).astype(BF16).astype(F32)
            ex[f, 0, 0:COLS, lanes] = g[0:32]
            ex[f, ROWS + 1, 0:COLS, lanes] = g[32:64]
            ex[f, :, COLS:PADDED, lanes] = g[64:144].reshape(ROWS + 2, 8, 256)
            return carry

        lax.fori_loop(0, INNER // 256, expand, 0, unroll=True)

    def filter_row(f, y):
        for i in range(INNER // 256):
            lanes = slice(i * 256, (i + 1) * 256)
            around = [ex[f, y + q, :, lanes] for q in range(3)]
            taps = [
                sum(around[q] * dw_ref[q, s : s + 1, lanes] for q in range(3)) for s in range(3)
            ]
            total = pltpu.roll(taps[0], 1, 0) + taps[1] + pltpu.roll(taps[2], PADDED - 1, 0)
            act[pl.ds(pl.multiple_of(y * COLS, COLS), COLS), lanes] = gelu(
                total[0:COLS] + db_ref[:, lanes]
            ).astype(BF16)

    def convolve(f, inner, p):
        first, last = (1, 1 + INNER_ROWS) if inner else (0, ROWS)

        def filter_rows(y, carry):
            filter_row(f, y)
            return carry

        lax.fori_loop(first, last, filter_rows, 0)
        cells = slice(first * COLS, last * COLS)
        kind = 0 if inner else 1
        for i in range(2):
            lanes = slice(i * 512, (i + 1) * 512)
            chosen_act[:, lanes] = matmul(choose[kind, :, cells], act[cells, lanes]).astype(BF16)
        for i in range(2):
            lanes = slice(i * 256, (i + 1) * 256)
            residual = matmul(choose[kind], xb[f, :, :, lanes].reshape(CELLS, 256))
            conv[p, :, lanes] = (residual + matmul(chosen_act[...], wp[:, lanes])).astype(BF16)
        for i in range(2):
            rows = slice(i * 64, (i + 1) * 64)
            att[p, rows] = layer_norm(conv[p, rows].astype(F32), gain).astype(BF16)

    convolve(0, True, 0)
    pl.semaphore_wait(barrier, 2 * (SIDE - 1) + 6)
    exchange(0, 0, att, mid, along_rows, a)

    loads[10].wait()
    place = iota((96, 1), 0)
    piece, index = place >> 4, place & 15
    cell_f = jnp.where(piece < 2, index >> 3, index & 1)
    cell_y = jnp.where(piece < 2, index & 7, jnp.where(piece < 4, 0, 7))
    cell_x = (piece & 1) * 31
    chosen = iota((96, 512), 1) == cell_f * CELLS + cell_y * COLS + cell_x
    edge[...] = matmul(one_hot(chosen), xb[...].reshape(512, WIDTH)).astype(BF16).reshape(6, 16, WIDTH)
    for copy in halos:
        copy.start()
    expand_tile(1)
    convolve(1, True, 1)
    exchange(0, 1, att, mid, along_rows, a)

    for copy in halos:
        copy.wait_recv()

    def convolve_outer(f, carry):
        expand_halo(f)
        convolve(f, False, FORECASTS + f)
        exchange(0, FORECASTS + f, att, mid, along_rows, a)
        return carry

    lax.fori_loop(0, FORECASTS, convolve_outer, 0)

    row, col = iota((PART, 1), 0), iota((PART, PART), 1)
    orders[0] = one_hot(col == ((row >> 4) << 1) + (((row & 15) >> 1) << 4) + (row & 1))
    orders[1] = one_hot(col == ((row & 7) << 4) + (((row & 63) >> 3) << 1) + (row >> 6))
    orders[2] = one_hot(col == ((row & 1) << 6) + (((row & 15) >> 1) << 3) + (row >> 4))

    def reorder(i, v):
        return matmul(orders[i], v).astype(BF16)

    def pass_on(p):
        wait_all(mid, p, received.at[0, p])
        mid_out[p] = reorder(0, mid[p])
        exchange(1, p, mid_out, owned, along_cols, c)

    pass_on(0)

    loads[7].wait()
    flat[...] = jnp.zeros_like(flat)
    total = jnp.zeros((16, 256), F32)
    for q in range(15):
        flat[:, 0:15] = table_ref[q]
        total = total + (pltpu.roll(flat[...], 16 * q, 1) if q else flat[...])
    flat[...] = total

    def shift(h, carry):
        row = jnp.broadcast_to(flat[pl.ds(h, 1), :], (8, 256))
        for i in range(SIDE):
            moved = pltpu.roll(row, 137 + 16 * i, 1, stride=1, stride_axis=0)
            shifted[h, i * 8 : (i + 1) * 8] = moved[:, 0:128]
        return carry

    lax.fori_loop(0, 16, shift, 0, unroll=True)
    target = iota((1, 256), 1)
    lane = ((target >> 6) << 7) + (((target & 63) >> 3) << 4) + (target & 7)
    spread = one_hot(iota((512, 256), 0) == lane)

    def set_bias(q, carry):
        rest = jnp.concatenate([shifted[q * 4 + h] for h in range(4)], axis=1)
        parts = []
        for _ in range(3):
            parts.append(rest.astype(BF16))
            rest = rest - parts[-1].astype(F32)
        total = matmul(jnp.concatenate(parts, axis=0), spread)
        bias[q] = (total[0:64] + total[64:128] + total[128:192]) * LOG2E
        return carry

    lax.fori_loop(0, QUADS, set_bias, 0)
    loads[8].wait()

    head = iota((1, 128), 1) >> 5
    own_lanes = [head == h for h in range(4)]

    def attend(p):
        wait_all(owned, p, received.at[1, p])
        xg[...] = reorder(1, owned[p])

        def project(i, carry):
            lanes = pl.ds(pl.multiple_of(i * 256, 256), 256)
            qkv[:, lanes] = matmul(xg[...], wqkv[:, lanes]).astype(BF16)
            return carry

        lax.fori_loop(0, 6, project, 0, unroll=True)

        for t in range(GROUPS):
            rows = slice(t * 64, (t + 1) * 64)
            for q in range(QUADS):
                lanes = slice(q * 128, (q + 1) * 128)
                query = qkv[rows, lanes]
                keys = qkv[rows, 512 + q * 128 : 640 + q * 128]
                values = qkv[rows, 1024 + q * 128 : 1152 + q * 128]
                apart = jnp.concatenate([query * one_hot(own_lanes[h]) for h in range(4)], axis=0)
                scores = lax.dot_general(
                    keys, apart, (((1,), (1,)), ((), ())), preferred_element_type=F32
                )
                scores = scores * (32**-0.5 * LOG2E) + bias[q]
                powers = jnp.exp2(scores - jnp.max(scores, axis=0, keepdims=True))
                share = 1.0 / jnp.sum(powers, axis=0, keepdims=True)
                attention = (powers * share).astype(BF16)
                mixed = lax.dot_general(
                    attention, values, (((0,), (0,)), ((), ())), preferred_element_type=F32
                )
                total = jnp.where(own_lanes[0], mixed[0:64], 0.0)
                for h in range(1, 4):
                    total = jnp.where(own_lanes[h], mixed[h * 64 : (h + 1) * 64], total)
                context[rows, lanes] = total.astype(BF16)

        answers[p] = reorder(2, context[...])
        exchange(2, p, answers, mid_back, along_cols, c)

    def pass_back(p):
        wait_all(mid_back, p, received.at[2, p])
        mid_return[p] = reorder(0, mid_back[p])

        def send(k, carry):
            @pl.when(k != a)
            def _():
                pltpu.make_async_remote_copy(
                    src_ref=mid_return.at[p, block(k)],
                    dst_ref=returned.at[p, block(a)],
                    send_sem=sent.at[3, p],
                    recv_sem=received.at[3, p],
                    device_id=(k * SIDE + m, c),
                    device_id_type=MESH,
                ).start()

            return carry

        lax.fori_loop(0, SIDE, send, 0)
        returned[p, block(a)] = mid_return[p, block(a)]

    def step(i, carry):
        @pl.when(i < PARTS)
        def _():
            pass_on(i)

        @pl.when(i <= PARTS)
        def _():
            attend(i - 1)

        @pl.when(i >= 2)
        def _():
            pass_back(i - 2)

        return carry

    lax.fori_loop(1, PARTS + 2, step, 0)
    loads[9].wait()
    for i in range(2):
        restore[i] = one_hot(iota((CELLS, PART), 1) == place_of(i == 0, iota((CELLS, 1), 0)))

    def finish(p, carry):
        wait_all(returned, p, received.at[3, p])
        f, kind = p % FORECASTS, p // FORECASTS
        for i in range(2):
            lanes = slice(i * 256, (i + 1) * 256)
            total = conv[p, :, lanes].astype(F32) + matmul(returned[p], wo[:, lanes])
            placed = matmul(restore[kind], total.astype(BF16))

            @pl.when(kind == 0)
            def _():
                finished[f, :, lanes] = placed

            @pl.when(kind == 1)
            def _():
                out_ref[f, :, :, lanes] = (
                    (finished[f, :, lanes] + placed).astype(BF16).reshape(ROWS, COLS, 256)
                )

        return carry

    lax.fori_loop(0, PARTS, finish, 0)

    for copy in halos:
        copy.wait_send()

    def drain(p, carry):
        for stage, ref in enumerate((att, mid_out, answers, mid_return)):
            wait_all(ref, p, sent.at[stage, p])
        return carry

    lax.fori_loop(0, PARTS, drain, 0)


def on_device(
    atmosphere_variables,
    premix_gain_vector,
    expand_weight,
    depth_weight,
    depth_bias,
    project_weight,
    norm_attn,
    qkv_weight,
    out_weight,
    bias_table,
):
    whole = pl.BlockSpec(memory_space=pltpu.HBM)
    tile = (FORECASTS, ROWS, COLS, WIDTH)
    parts = pltpu.VMEM((PARTS, PART, WIDTH), BF16)
    return pl.pallas_call(
        kernel,
        out_shape=pltpu.VMEM(tile, BF16),
        in_specs=[whole] * 10,
        out_specs=pl.BlockSpec(memory_space=pltpu.VMEM),
        scratch_shapes=[
            pltpu.VMEM(tile, BF16),
            pltpu.VMEM((1, WIDTH), F32),
            pltpu.VMEM((WIDTH, INNER), BF16),
            pltpu.VMEM((3, 3, INNER), F32),
            pltpu.VMEM((1, INNER), F32),
            pltpu.VMEM((INNER, WIDTH), BF16),
            pltpu.VMEM((1, WIDTH), F32),
            pltpu.VMEM((WIDTH, 3 * WIDTH), BF16),
            pltpu.VMEM((WIDTH, WIDTH), BF16),
            pltpu.VMEM((15, 16, 15), F32),
            pltpu.VMEM((6, 16, WIDTH), BF16),
            pltpu.VMEM((2, FORECASTS, COLS, WIDTH), BF16),
            pltpu.VMEM((6, 16, WIDTH), BF16),
            pltpu.VMEM((CELLS, WIDTH), BF16),
            pltpu.VMEM((FORECASTS, ROWS + 2, PADDED, INNER), F32),
            pltpu.VMEM((CELLS, INNER), BF16),
            pltpu.VMEM((PART, INNER), BF16),
            parts,
            pltpu.VMEM((2, PART, CELLS), BF16),
            pltpu.VMEM((2, CELLS, PART), BF16),
            pltpu.VMEM((FORECASTS, CELLS, WIDTH), F32),
            *[parts] * 8,
            pltpu.VMEM((3, PART, PART), BF16),
            pltpu.VMEM((PART, WIDTH), BF16),
            pltpu.VMEM((PART, 3 * WIDTH), BF16),
            pltpu.VMEM((PART, WIDTH), BF16),
            pltpu.VMEM((16, 256), F32),
            pltpu.VMEM((16, MEMBERS, 128), F32),
            pltpu.VMEM((QUADS, MEMBERS, 256), F32),
            pltpu.SemaphoreType.DMA((11,)),
            pltpu.SemaphoreType.DMA((8,)),
            pltpu.SemaphoreType.DMA((8,)),
            pltpu.SemaphoreType.DMA((4, PARTS)),
            pltpu.SemaphoreType.DMA((4, PARTS)),
        ],
        compiler_params=pltpu.CompilerParams(
            collective_id=0, has_side_effects=True, vmem_limit_bytes=56 * 1024 * 1024
        ),
        name="maxvit_layer",
    )(
        atmosphere_variables,
        premix_gain_vector.reshape(1, WIDTH),
        expand_weight,
        depth_weight,
        depth_bias.reshape(1, INNER),
        project_weight,
        norm_attn.reshape(1, WIDTH),
        qkv_weight,
        out_weight,
        bias_table.transpose(1, 0, 2),
    )


def solution(mesh):
    return jax.shard_map(
        on_device,
        mesh=mesh,
        in_specs=(P(None, "rows", "cols", None), P(), P(), P(), P(), P(), P(), P(), P(), P()),
        out_specs=P(None, "rows", "cols", None),
        check_vma=False,
    )
```

```python
import jax
import jax.numpy as jnp
from jax import lax
from jax.experimental import pallas as pl
from jax.experimental.pallas import tpu as pltpu
from jax.sharding import PartitionSpec as P

MESH = pl.DeviceIdType.MESH
F32 = jnp.float32
BF16 = jnp.bfloat16

FORECASTS = 2
ROWS = 8
COLS = 32
CELLS = ROWS * COLS
WIDTH = 512
INNER = 1024
SIDE = 8
PARTS = 4
PART = FORECASTS * CELLS // PARTS
INNER_ROWS = 5
PIECE = PART // SIDE
GROUPS = PIECE // SIDE
MEMBERS = SIDE * SIDE
PADDED = 40
QUADS = 4
LOG2E = 1.4426950408889634


def gelu(v):
    half = 0.5 * v
    return half + half * jnp.tanh(v * (0.7978845608028654 + 0.035677408136300125 * (v * v)))


def layer_norm(v, gain):
    centred = v - jnp.mean(v, axis=-1, keepdims=True)
    variance = jnp.mean(centred * centred, axis=-1, keepdims=True)
    return centred * lax.rsqrt(variance + 1e-05) * gain


def iota(shape, dim):
    return lax.broadcasted_iota(jnp.int32, shape, dim)


def one_hot(condition):
    return jnp.where(condition, 1.0, 0.0).astype(BF16)


def place_of(inner, cell):
    y, x = cell >> 5, cell & 31
    if inner:
        k = (y - 1) * 30 + x - 1
        return jnp.where((y > 0) & (y < 6) & (x > 0) & (x < 31) & (k < PART), k, -1)
    sides = jnp.where(x == 0, 2 * y + 30, jnp.where(x == 31, 2 * y + 31, -1))
    fifth = jnp.where(x == 0, 40, jnp.where(x > 8, 32 + x, -1))
    return jnp.where(
        y == 0, x, jnp.where(y < 5, sides, jnp.where(y == 5, fifth, cell - (CELLS - PART)))
    )


def matmul(a, b):
    return jnp.dot(a, b, preferred_element_type=F32)


def kernel(
    x_hbm, premix_hbm, we_hbm, dw_hbm, db_hbm, wp_hbm, gain_hbm, wqkv_hbm, wo_hbm, table_hbm,
    out_ref,
    xb, premix_ref, we, dw_ref, db_ref, wp, gain_ref, wqkv, wo, table_ref,
    edge, halo_rows, halo_edge, normed, ex, act, chosen_act, conv, choose, restore, finished,
    att, mid, mid_out, owned, answers, mid_back, mid_return, returned,
    orders, xg, qkv, context, flat, shifted, bias,
    load_sem, halo_send, halo_recv, sent, received,
):
    r = lax.axis_index("rows")
    c = lax.axis_index("cols")
    n_rows = lax.axis_size("rows")
    n_cols = lax.axis_size("cols")
    a, m = r // SIDE, r % SIDE

    loads = [
        pltpu.make_async_copy(src, dst, load_sem.at[i])
        for i, (src, dst) in enumerate(
            (
                (x_hbm.at[0], xb.at[0]), (premix_hbm, premix_ref), (we_hbm, we), (dw_hbm, dw_ref),
                (db_hbm, db_ref), (wp_hbm, wp), (gain_hbm, gain_ref), (table_hbm, table_ref),
                (wqkv_hbm, wqkv), (wo_hbm, wo), (x_hbm.at[1], xb.at[1]),
            )
        )
    ]
    for load in loads[:3]:
        load.start()

    north, south = lax.rem(r + n_rows - 1, n_rows), lax.rem(r + 1, n_rows)
    west, east = lax.rem(c + n_cols - 1, n_cols), lax.rem(c + 1, n_cols)

    def along_rows(k):
        other = lax.rem(a + k, SIDE)
        return other, (other * SIDE + m, c)

    def along_cols(k):
        other = lax.rem(c + k, SIDE)
        return other, (r, other)

    barrier = pltpu.get_barrier_semaphore()
    for place in (
        (north, c), (south, c), (north, west), (north, east), (south, west), (south, east),
    ):
        pl.semaphore_signal(barrier, inc=1, device_id=place, device_id_type=MESH)

    def greet(k, carry):
        for along in (along_cols, along_rows):
            pl.semaphore_signal(barrier, inc=1, device_id=along(k)[1], device_id_type=MESH)
        return carry

    lax.fori_loop(1, SIDE, greet, 0)

    def halo(i, src, dst, row, col):
        return pltpu.make_async_remote_copy(
            src_ref=src,
            dst_ref=dst,
            send_sem=halo_send.at[i],
            recv_sem=halo_recv.at[i],
            device_id=(row, col),
            device_id_type=MESH,
        )

    halos = [
        halo(0, xb.at[:, ROWS - 1], halo_rows.at[0], south, c),
        halo(1, xb.at[:, 0], halo_rows.at[1], north, c),
        halo(2, edge.at[0], halo_edge.at[0], r, west),
        halo(3, edge.at[1], halo_edge.at[1], r, east),
        halo(4, edge.at[5], halo_edge.at[2], south, east),
        halo(5, edge.at[4], halo_edge.at[3], south, west),
        halo(6, edge.at[3], halo_edge.at[4], north, east),
        halo(7, edge.at[2], halo_edge.at[5], north, west),
    ]
    def block(k):
        return pl.ds(pl.multiple_of(k * PIECE, PIECE), PIECE)

    def exchange(stage, p, src, dst, along, mine):
        def send(n, carry):
            k = SIDE // 2 + jnp.where(n % 2 == 1, -(n // 2), n // 2)
            other, place = along(k)
            pltpu.make_async_remote_copy(
                src_ref=src.at[p, block(other)],
                dst_ref=dst.at[p, block(mine)],
                send_sem=sent.at[stage, p],
                recv_sem=received.at[stage, p],
                device_id=place,
                device_id_type=MESH,
            ).start()
            return carry

        lax.fori_loop(1, SIDE, send, 0)
        dst[p, block(mine)] = src[p, block(mine)]

    def wait_all(ref, p, sem):
        others = ref.at[p, pl.ds(0, PART - PIECE)]
        pltpu.make_async_copy(others, others, sem).wait()

    def expand_tile(f):
        def norm_rows(i, carry):
            v = xb[f, pl.ds(2 * i, 2)].astype(F32).reshape(64, WIDTH)
            normed[pl.ds(pl.multiple_of(i * 64, 64), 64)] = layer_norm(v, premix).astype(BF16)
            return carry

        lax.fori_loop(0, 4, norm_rows, 0, unroll=True)

        def expand(i, carry):
            lanes = pl.ds(pl.multiple_of(i * 256, 256), 256)
            g = gelu(matmul(normed[0:CELLS], we[:, lanes])).astype(BF16).astype(F32)
            ex[f, 1 : ROWS + 1, 0:COLS, lanes] = g.reshape(ROWS, COLS, 256)
            return carry

        lax.fori_loop(0, INNER // 256, expand, 0, unroll=True)

    for f in range(FORECASTS):
        ex[f, :, COLS:PADDED] = jnp.zeros((ROWS + 2, PADDED - COLS, INNER), F32)
    for i in range(2):
        choose[i] = one_hot(iota((PART, CELLS), 0) == place_of(i == 0, iota((1, CELLS), 1)))
    loads[0].wait()
    for load in loads[3:]:
        load.start()
    loads[1].wait()
    premix = premix_ref[...]
    loads[2].wait()
    expand_tile(0)
    for load in loads[3:7]:
        load.wait()
    gain = gain_ref[...]

    def expand_halo(f):
        top = halo_rows[0, f].astype(F32) * jnp.where(r == 0, 0.0, 1.0)
        bottom = halo_rows[1, f].astype(F32) * jnp.where(r == n_rows - 1, 0.0, 1.0)
        normed[0:32] = layer_norm(top, premix).astype(BF16)
        normed[32:64] = layer_norm(bottom, premix).astype(BF16)
        place = iota((80, 1), 0)
        y, slot = place >> 3, place & 7
        inside = ((y > 0) | (r > 0)) & ((y < 9) | (r < n_rows - 1))
        in_east = (slot == 0) & (c < n_cols - 1)
        in_west = (slot == 7) & (c > 0)
        source_east = jnp.where(y == 0, 48 + f, jnp.where(y == 9, 80 + f, f * 8 + y - 1))
        source_west = jnp.where(y == 0, 32 + f, jnp.where(y == 9, 64 + f, 16 + f * 8 + y - 1))
        source = jnp.where(in_east, source_east, source_west)
        source = jnp.where(inside & (in_east | in_west), source, -1)
        chosen = iota((80, 96), 1) == source
        sides = matmul(one_hot(chosen), halo_edge[...].reshape(96, WIDTH))
        normed[64:144] = layer_norm(sides, premix).astype(BF16)

        def expand(i, carry):
            lanes = pl.ds(pl.multiple_of(i * 256, 256), 256)
            g = gelu(matmul(normed[0:144], we[:, lanes])).astype(BF16).astype(F32)
            ex[f, 0, 0:COLS, lanes] = g[0:32]
            ex[f, ROWS + 1, 0:COLS, lanes] = g[32:64]
            ex[f, :, COLS:PADDED, lanes] = g[64:144].reshape(ROWS + 2, 8, 256)
            return carry

        lax.fori_loop(0, INNER // 256, expand, 0, unroll=True)

    def filter_row(f, y):
        for i in range(INNER // 256):
            lanes = slice(i * 256, (i + 1) * 256)
            around = [ex[f, y + q, :, lanes] for q in range(3)]
            taps = [
                sum(around[q] * dw_ref[q, s : s + 1, lanes] for q in range(3)) for s in range(3)
            ]
            total = pltpu.roll(taps[0], 1, 0) + taps[1] + pltpu.roll(taps[2], PADDED - 1, 0)
            act[pl.ds(pl.multiple_of(y * COLS, COLS), COLS), lanes] = gelu(
                total[0:COLS] + db_ref[:, lanes]
            ).astype(BF16)

    def convolve(f, inner, p):
        first, last = (1, 1 + INNER_ROWS) if inner else (0, ROWS)

        def filter_rows(y, carry):
            filter_row(f, y)
            return carry

        lax.fori_loop(first, last, filter_rows, 0)
        cells = slice(first * COLS, last * COLS)
        kind = 0 if inner else 1
        for i in range(2):
            lanes = slice(i * 512, (i + 1) * 512)
            chosen_act[:, lanes] = matmul(choose[kind, :, cells], act[cells, lanes]).astype(BF16)
        for i in range(2):
            lanes = slice(i * 256, (i + 1) * 256)
            residual = matmul(choose[kind], xb[f, :, :, lanes].reshape(CELLS, 256))
            conv[p, :, lanes] = (residual + matmul(chosen_act[...], wp[:, lanes])).astype(BF16)
        for i in range(2):
            rows = slice(i * 64, (i + 1) * 64)
            att[p, rows] = layer_norm(conv[p, rows].astype(F32), gain).astype(BF16)

    convolve(0, True, 0)
    pl.semaphore_wait(barrier, 2 * (SIDE - 1) + 6)
    exchange(0, 0, att, mid, along_rows, a)

    loads[10].wait()
    place = iota((96, 1), 0)
    piece, index = place >> 4, place & 15
    cell_f = jnp.where(piece < 2, index >> 3, index & 1)
    cell_y = jnp.where(piece < 2, index & 7, jnp.where(piece < 4, 0, 7))
    cell_x = (piece & 1) * 31
    chosen = iota((96, 512), 1) == cell_f * CELLS + cell_y * COLS + cell_x
    edge[...] = matmul(one_hot(chosen), xb[...].reshape(512, WIDTH)).astype(BF16).reshape(6, 16, WIDTH)
    for copy in halos:
        copy.start()
    expand_tile(1)
    convolve(1, True, 1)
    exchange(0, 1, att, mid, along_rows, a)

    for copy in halos:
        copy.wait_recv()

    def convolve_outer(f, carry):
        expand_halo(f)
        convolve(f, False, FORECASTS + f)
        exchange(0, FORECASTS + f, att, mid, along_rows, a)
        return carry

    lax.fori_loop(0, FORECASTS, convolve_outer, 0)

    row, col = iota((PART, 1), 0), iota((PART, PART), 1)
    orders[0] = one_hot(col == ((row >> 4) << 1) + (((row & 15) >> 1) << 4) + (row & 1))
    orders[1] = one_hot(col == ((row & 7) << 4) + (((row & 63) >> 3) << 1) + (row >> 6))
    orders[2] = one_hot(col == ((row & 1) << 6) + (((row & 15) >> 1) << 3) + (row >> 4))

    def reorder(i, v):
        return matmul(orders[i], v).astype(BF16)

    def pass_on(p):
        wait_all(mid, p, received.at[0, p])
        mid_out[p] = reorder(0, mid[p])
        exchange(1, p, mid_out, owned, along_cols, c)

    pass_on(0)

    loads[7].wait()
    flat[...] = jnp.zeros_like(flat)
    total = jnp.zeros((16, 256), F32)
    for q in range(15):
        flat[:, 0:15] = table_ref[q]
        total = total + (pltpu.roll(flat[...], 16 * q, 1) if q else flat[...])
    flat[...] = total

    def shift(h, carry):
        row = jnp.broadcast_to(flat[pl.ds(h, 1), :], (8, 256))
        for i in range(SIDE):
            moved = pltpu.roll(row, 137 + 16 * i, 1, stride=1, stride_axis=0)
            shifted[h, i * 8 : (i + 1) * 8] = moved[:, 0:128]
        return carry

    lax.fori_loop(0, 16, shift, 0, unroll=True)
    target = iota((1, 256), 1)
    lane = ((target >> 6) << 7) + (((target & 63) >> 3) << 4) + (target & 7)
    spread = one_hot(iota((512, 256), 0) == lane)

    def set_bias(q, carry):
        rest = jnp.concatenate([shifted[q * 4 + h] for h in range(4)], axis=1)
        parts = []
        for _ in range(3):
            parts.append(rest.astype(BF16))
            rest = rest - parts[-1].astype(F32)
        total = matmul(jnp.concatenate(parts, axis=0), spread)
        bias[q] = (total[0:64] + total[64:128] + total[128:192]) * LOG2E
        return carry

    lax.fori_loop(0, QUADS, set_bias, 0)
    loads[8].wait()

    head = iota((1, 128), 1) >> 5
    own_lanes = [head == h for h in range(4)]

    def attend(p):
        wait_all(owned, p, received.at[1, p])
        xg[...] = reorder(1, owned[p])

        def project(i, carry):
            lanes = pl.ds(pl.multiple_of(i * 256, 256), 256)
            qkv[:, lanes] = matmul(xg[...], wqkv[:, lanes]).astype(BF16)
            return carry

        lax.fori_loop(0, 6, project, 0, unroll=True)

        for t in range(GROUPS):
            rows = slice(t * 64, (t + 1) * 64)
            for q in range(QUADS):
                lanes = slice(q * 128, (q + 1) * 128)
                query = qkv[rows, lanes]
                keys = qkv[rows, 512 + q * 128 : 640 + q * 128]
                values = qkv[rows, 1024 + q * 128 : 1152 + q * 128]
                apart = jnp.concatenate([query * one_hot(own_lanes[h]) for h in range(4)], axis=0)
                scores = lax.dot_general(
                    keys, apart, (((1,), (1,)), ((), ())), preferred_element_type=F32
                )
                scores = scores * (32**-0.5 * LOG2E) + bias[q]
                powers = jnp.exp2(scores - jnp.max(scores, axis=0, keepdims=True))
                share = 1.0 / jnp.sum(powers, axis=0, keepdims=True)
                attention = (powers * share).astype(BF16)
                mixed = lax.dot_general(
                    attention, values, (((0,), (0,)), ((), ())), preferred_element_type=F32
                )
                total = jnp.where(own_lanes[0], mixed[0:64], 0.0)
                for h in range(1, 4):
                    total = jnp.where(own_lanes[h], mixed[h * 64 : (h + 1) * 64], total)
                context[rows, lanes] = total.astype(BF16)

        answers[p] = reorder(2, context[...])
        exchange(2, p, answers, mid_back, along_cols, c)

    def pass_back(p):
        wait_all(mid_back, p, received.at[2, p])
        mid_return[p] = reorder(0, mid_back[p])

        def send(k, carry):
            @pl.when(k != a)
            def _():
                pltpu.make_async_remote_copy(
                    src_ref=mid_return.at[p, block(k)],
                    dst_ref=returned.at[p, block(a)],
                    send_sem=sent.at[3, p],
                    recv_sem=received.at[3, p],
                    device_id=(k * SIDE + m, c),
                    device_id_type=MESH,
                ).start()

            return carry

        lax.fori_loop(0, SIDE, send, 0)
        returned[p, block(a)] = mid_return[p, block(a)]

    def step(i, carry):
        @pl.when(i < PARTS)
        def _():
            pass_on(i)

        @pl.when(i <= PARTS)
        def _():
            attend(i - 1)

        @pl.when(i >= 2)
        def _():
            pass_back(i - 2)

        return carry

    lax.fori_loop(1, PARTS + 2, step, 0)
    loads[9].wait()
    for i in range(2):
        restore[i] = one_hot(iota((CELLS, PART), 1) == place_of(i == 0, iota((CELLS, 1), 0)))

    for copy in halos:
        copy.wait_send()

    def drain(p, carry):
        for stage, ref in enumerate((att, mid_out, answers)):
            wait_all(ref, p, sent.at[stage, p])
        return carry

    lax.fori_loop(0, PARTS, drain, 0)

    def finish(p, carry):
        wait_all(returned, p, received.at[3, p])
        f, kind = p % FORECASTS, p // FORECASTS
        total = conv[p].astype(F32) + matmul(returned[p], wo[...])
        placed = matmul(restore[kind], total.astype(BF16))

        @pl.when(kind == 0)
        def _():
            finished[f] = placed

        @pl.when(kind == 1)
        def _():
            out_ref[f] = (finished[f] + placed).astype(BF16).reshape(ROWS, COLS, WIDTH)

        return carry

    lax.fori_loop(0, PARTS, finish, 0)

    def drain_back(p, carry):
        wait_all(mid_return, p, sent.at[3, p])
        return carry

    lax.fori_loop(0, PARTS, drain_back, 0)


def on_device(
    atmosphere_variables,
    premix_gain_vector,
    expand_weight,
    depth_weight,
    depth_bias,
    project_weight,
    norm_attn,
    qkv_weight,
    out_weight,
    bias_table,
):
    whole = pl.BlockSpec(memory_space=pltpu.HBM)
    tile = (FORECASTS, ROWS, COLS, WIDTH)
    parts = pltpu.VMEM((PARTS, PART, WIDTH), BF16)
    return pl.pallas_call(
        kernel,
        out_shape=pltpu.VMEM(tile, BF16),
        in_specs=[whole] * 10,
        out_specs=pl.BlockSpec(memory_space=pltpu.VMEM),
        scratch_shapes=[
            pltpu.VMEM(tile, BF16),
            pltpu.VMEM((1, WIDTH), F32),
            pltpu.VMEM((WIDTH, INNER), BF16),
            pltpu.VMEM((3, 3, INNER), F32),
            pltpu.VMEM((1, INNER), F32),
            pltpu.VMEM((INNER, WIDTH), BF16),
            pltpu.VMEM((1, WIDTH), F32),
            pltpu.VMEM((WIDTH, 3 * WIDTH), BF16),
            pltpu.VMEM((WIDTH, WIDTH), BF16),
            pltpu.VMEM((15, 16, 15), F32),
            pltpu.VMEM((6, 16, WIDTH), BF16),
            pltpu.VMEM((2, FORECASTS, COLS, WIDTH), BF16),
            pltpu.VMEM((6, 16, WIDTH), BF16),
            pltpu.VMEM((CELLS, WIDTH), BF16),
            pltpu.VMEM((FORECASTS, ROWS + 2, PADDED, INNER), F32),
            pltpu.VMEM((CELLS, INNER), BF16),
            pltpu.VMEM((PART, INNER), BF16),
            parts,
            pltpu.VMEM((2, PART, CELLS), BF16),
            pltpu.VMEM((2, CELLS, PART), BF16),
            pltpu.VMEM((FORECASTS, CELLS, WIDTH), F32),
            *[parts] * 8,
            pltpu.VMEM((3, PART, PART), BF16),
            pltpu.VMEM((PART, WIDTH), BF16),
            pltpu.VMEM((PART, 3 * WIDTH), BF16),
            pltpu.VMEM((PART, WIDTH), BF16),
            pltpu.VMEM((16, 256), F32),
            pltpu.VMEM((16, MEMBERS, 128), F32),
            pltpu.VMEM((QUADS, MEMBERS, 256), F32),
            pltpu.SemaphoreType.DMA((11,)),
            pltpu.SemaphoreType.DMA((8,)),
            pltpu.SemaphoreType.DMA((8,)),
            pltpu.SemaphoreType.DMA((4, PARTS)),
            pltpu.SemaphoreType.DMA((4, PARTS)),
        ],
        compiler_params=pltpu.CompilerParams(
            collective_id=0, has_side_effects=True, vmem_limit_bytes=56 * 1024 * 1024
        ),
        name="maxvit_layer",
    )(
        atmosphere_variables,
        premix_gain_vector.reshape(1, WIDTH),
        expand_weight,
        depth_weight,
        depth_bias.reshape(1, INNER),
        project_weight,
        norm_attn.reshape(1, WIDTH),
        qkv_weight,
        out_weight,
        bias_table.transpose(1, 0, 2),
    )


def solution(mesh):
    return jax.shard_map(
        on_device,
        mesh=mesh,
        in_specs=(P(None, "rows", "cols", None), P(), P(), P(), P(), P(), P(), P(), P(), P()),
        out_specs=P(None, "rows", "cols", None),
        check_vma=False,
    )
```

```python
import jax
import jax.numpy as jnp
from jax import lax
from jax.experimental import pallas as pl
from jax.experimental.pallas import tpu as pltpu
from jax.sharding import PartitionSpec as P

MESH = pl.DeviceIdType.MESH
F32 = jnp.float32
BF16 = jnp.bfloat16

FORECASTS = 2
ROWS = 8
COLS = 32
CELLS = ROWS * COLS
WIDTH = 512
INNER = 1024
SIDE = 8
PARTS = 4
PART = FORECASTS * CELLS // PARTS
INNER_ROWS = 5
PIECE = PART // SIDE
GROUPS = PIECE // SIDE
MEMBERS = SIDE * SIDE
PADDED = 40
QUADS = 4
LOG2E = 1.4426950408889634


def gelu(v):
    half = 0.5 * v
    return half + half * jnp.tanh(v * (0.7978845608028654 + 0.035677408136300125 * (v * v)))


def layer_norm(v, gain):
    centred = v - jnp.mean(v, axis=-1, keepdims=True)
    variance = jnp.mean(centred * centred, axis=-1, keepdims=True)
    return centred * lax.rsqrt(variance + 1e-05) * gain


def iota(shape, dim):
    return lax.broadcasted_iota(jnp.int32, shape, dim)


def one_hot(condition):
    return jnp.where(condition, 1.0, 0.0).astype(BF16)


def place_of(inner, cell):
    y, x = cell >> 5, cell & 31
    if inner:
        k = (y - 1) * 30 + x - 1
        return jnp.where((y > 0) & (y < 6) & (x > 0) & (x < 31) & (k < PART), k, -1)
    sides = jnp.where(x == 0, 2 * y + 30, jnp.where(x == 31, 2 * y + 31, -1))
    fifth = jnp.where(x == 0, 40, jnp.where(x > 8, 32 + x, -1))
    return jnp.where(
        y == 0, x, jnp.where(y < 5, sides, jnp.where(y == 5, fifth, cell - (CELLS - PART)))
    )


def matmul(a, b):
    return jnp.dot(a, b, preferred_element_type=F32)


def kernel(
    x_hbm, premix_hbm, we_hbm, dw_hbm, db_hbm, wp_hbm, gain_hbm, wqkv_hbm, wo_hbm, table_hbm,
    out_ref,
    xb, premix_ref, we, dw_ref, db_ref, wp, gain_ref, wqkv, wo, table_ref,
    edge, halo_rows, halo_edge, normed, ex, act, chosen_act, conv, choose, restore, finished,
    att, mid, mid_out, owned, answers, mid_back, mid_return, returned,
    orders, xg, qkv, context, flat, shifted, bias,
    load_sem, halo_send, halo_recv, sent, received,
):
    r = lax.axis_index("rows")
    c = lax.axis_index("cols")
    n_rows = lax.axis_size("rows")
    n_cols = lax.axis_size("cols")
    a, m = r // SIDE, r % SIDE

    loads = [
        pltpu.make_async_copy(src, dst, load_sem.at[i])
        for i, (src, dst) in enumerate(
            (
                (x_hbm.at[0], xb.at[0]), (premix_hbm, premix_ref), (we_hbm, we), (dw_hbm, dw_ref),
                (db_hbm, db_ref), (wp_hbm, wp), (gain_hbm, gain_ref), (table_hbm, table_ref),
                (wqkv_hbm, wqkv), (wo_hbm, wo), (x_hbm.at[1], xb.at[1]),
            )
        )
    ]
    for load in loads[:3]:
        load.start()

    north, south = lax.rem(r + n_rows - 1, n_rows), lax.rem(r + 1, n_rows)
    west, east = lax.rem(c + n_cols - 1, n_cols), lax.rem(c + 1, n_cols)

    def along_rows(k):
        other = lax.rem(a + k, SIDE)
        return other, (other * SIDE + m, c)

    def along_cols(k):
        other = lax.rem(c + k, SIDE)
        return other, (r, other)

    barrier = pltpu.get_barrier_semaphore()
    for place in (
        (north, c), (south, c), (north, west), (north, east), (south, west), (south, east),
    ):
        pl.semaphore_signal(barrier, inc=1, device_id=place, device_id_type=MESH)

    def greet(k, carry):
        for along in (along_cols, along_rows):
            pl.semaphore_signal(barrier, inc=1, device_id=along(k)[1], device_id_type=MESH)
        return carry

    lax.fori_loop(1, SIDE, greet, 0)

    def halo(i, src, dst, row, col):
        return pltpu.make_async_remote_copy(
            src_ref=src,
            dst_ref=dst,
            send_sem=halo_send.at[i],
            recv_sem=halo_recv.at[i],
            device_id=(row, col),
            device_id_type=MESH,
        )

    halos = [
        halo(0, xb.at[:, ROWS - 1], halo_rows.at[0], south, c),
        halo(1, xb.at[:, 0], halo_rows.at[1], north, c),
        halo(2, edge.at[0], halo_edge.at[0], r, west),
        halo(3, edge.at[1], halo_edge.at[1], r, east),
        halo(4, edge.at[5], halo_edge.at[2], south, east),
        halo(5, edge.at[4], halo_edge.at[3], south, west),
        halo(6, edge.at[3], halo_edge.at[4], north, east),
        halo(7, edge.at[2], halo_edge.at[5], north, west),
    ]
    def block(k):
        return pl.ds(pl.multiple_of(k * PIECE, PIECE), PIECE)

    def exchange(stage, p, src, dst, along, mine):
        def send(n, carry):
            k = SIDE // 2 + jnp.where(n % 2 == 1, -(n // 2), n // 2)
            other, place = along(k)
            pltpu.make_async_remote_copy(
                src_ref=src.at[p, block(other)],
                dst_ref=dst.at[p, block(mine)],
                send_sem=sent.at[stage, p],
                recv_sem=received.at[stage, p],
                device_id=place,
                device_id_type=MESH,
            ).start()
            return carry

        lax.fori_loop(1, SIDE, send, 0)
        dst[p, block(mine)] = src[p, block(mine)]

    def wait_all(ref, p, sem):
        others = ref.at[p, pl.ds(0, PART - PIECE)]
        pltpu.make_async_copy(others, others, sem).wait()

    def expand_tile(f):
        def norm_rows(i, carry):
            v = xb[f, pl.ds(2 * i, 2)].astype(F32).reshape(64, WIDTH)
            normed[pl.ds(pl.multiple_of(i * 64, 64), 64)] = layer_norm(v, premix).astype(BF16)
            return carry

        lax.fori_loop(0, 4, norm_rows, 0, unroll=True)

        def expand(i, carry):
            lanes = pl.ds(pl.multiple_of(i * 256, 256), 256)
            g = gelu(matmul(normed[0:CELLS], we[:, lanes])).astype(BF16).astype(F32)
            ex[f, 1 : ROWS + 1, 0:COLS, lanes] = g.reshape(ROWS, COLS, 256)
            return carry

        lax.fori_loop(0, INNER // 256, expand, 0, unroll=True)

    for f in range(FORECASTS):
        ex[f, :, COLS:PADDED] = jnp.zeros((ROWS + 2, PADDED - COLS, INNER), F32)
    for i in range(2):
        choose[i] = one_hot(iota((PART, CELLS), 0) == place_of(i == 0, iota((1, CELLS), 1)))
    loads[0].wait()
    for load in loads[3:]:
        load.start()
    loads[1].wait()
    premix = premix_ref[...]
    loads[2].wait()
    expand_tile(0)
    for load in loads[3:7]:
        load.wait()
    gain = gain_ref[...]

    def expand_halo(f):
        top = halo_rows[0, f].astype(F32) * jnp.where(r == 0, 0.0, 1.0)
        bottom = halo_rows[1, f].astype(F32) * jnp.where(r == n_rows - 1, 0.0, 1.0)
        normed[0:32] = layer_norm(top, premix).astype(BF16)
        normed[32:64] = layer_norm(bottom, premix).astype(BF16)
        place = iota((80, 1), 0)
        y, slot = place >> 3, place & 7
        inside = ((y > 0) | (r > 0)) & ((y < 9) | (r < n_rows - 1))
        in_east = (slot == 0) & (c < n_cols - 1)
        in_west = (slot == 7) & (c > 0)
        source_east = jnp.where(y == 0, 48 + f, jnp.where(y == 9, 80 + f, f * 8 + y - 1))
        source_west = jnp.where(y == 0, 32 + f, jnp.where(y == 9, 64 + f, 16 + f * 8 + y - 1))
        source = jnp.where(in_east, source_east, source_west)
        source = jnp.where(inside & (in_east | in_west), source, -1)
        chosen = iota((80, 96), 1) == source
        sides = matmul(one_hot(chosen), halo_edge[...].reshape(96, WIDTH))
        normed[64:144] = layer_norm(sides, premix).astype(BF16)

        def expand(i, carry):
            lanes = pl.ds(pl.multiple_of(i * 256, 256), 256)
            g = gelu(matmul(normed[0:144], we[:, lanes])).astype(BF16).astype(F32)
            ex[f, 0, 0:COLS, lanes] = g[0:32]
            ex[f, ROWS + 1, 0:COLS, lanes] = g[32:64]
            ex[f, :, COLS:PADDED, lanes] = g[64:144].reshape(ROWS + 2, 8, 256)
            return carry

        lax.fori_loop(0, INNER // 256, expand, 0, unroll=True)

    def filter_row(f, y):
        for i in range(INNER // 256):
            lanes = slice(i * 256, (i + 1) * 256)
            around = [ex[f, y + q, :, lanes] for q in range(3)]
            taps = [
                sum(around[q] * dw_ref[q, s : s + 1, lanes] for q in range(3)) for s in range(3)
            ]
            total = pltpu.roll(taps[0], 1, 0) + taps[1] + pltpu.roll(taps[2], PADDED - 1, 0)
            act[pl.ds(pl.multiple_of(y * COLS, COLS), COLS), lanes] = gelu(
                total[0:COLS] + db_ref[:, lanes]
            ).astype(BF16)

    def convolve(f, inner, p):
        first, last = (1, 1 + INNER_ROWS) if inner else (0, ROWS)

        def filter_rows(y, carry):
            filter_row(f, y)
            return carry

        lax.fori_loop(first, last, filter_rows, 0)
        cells = slice(first * COLS, last * COLS)
        kind = 0 if inner else 1
        for i in range(2):
            lanes = slice(i * 512, (i + 1) * 512)
            chosen_act[:, lanes] = matmul(choose[kind, :, cells], act[cells, lanes]).astype(BF16)
        for i in range(2):
            lanes = slice(i * 256, (i + 1) * 256)
            residual = matmul(choose[kind], xb[f, :, :, lanes].reshape(CELLS, 256))
            conv[p, :, lanes] = (residual + matmul(chosen_act[...], wp[:, lanes])).astype(BF16)
        for i in range(2):
            rows = slice(i * 64, (i + 1) * 64)
            att[p, rows] = layer_norm(conv[p, rows].astype(F32), gain).astype(BF16)

    convolve(0, True, 0)
    loads[10].wait()
    place = iota((96, 1), 0)
    piece, index = place >> 4, place & 15
    cell_f = jnp.where(piece < 2, index >> 3, index & 1)
    cell_y = jnp.where(piece < 2, index & 7, jnp.where(piece < 4, 0, 7))
    cell_x = (piece & 1) * 31
    chosen = iota((96, 512), 1) == cell_f * CELLS + cell_y * COLS + cell_x
    edge[...] = matmul(one_hot(chosen), xb[...].reshape(512, WIDTH)).astype(BF16).reshape(6, 16, WIDTH)
    pl.semaphore_wait(barrier, 2 * (SIDE - 1) + 6)
    for copy in halos:
        copy.start()
    exchange(0, 0, att, mid, along_rows, a)

    expand_tile(1)
    convolve(1, True, 1)
    exchange(0, 1, att, mid, along_rows, a)

    for copy in halos:
        copy.wait_recv()

    def convolve_outer(f, carry):
        expand_halo(f)
        convolve(f, False, FORECASTS + f)
        exchange(0, FORECASTS + f, att, mid, along_rows, a)
        return carry

    lax.fori_loop(0, FORECASTS, convolve_outer, 0)

    row, col = iota((PART, 1), 0), iota((PART, PART), 1)
    orders[0] = one_hot(col == ((row >> 4) << 1) + (((row & 15) >> 1) << 4) + (row & 1))
    orders[1] = one_hot(col == ((row & 7) << 4) + (((row & 63) >> 3) << 1) + (row >> 6))
    orders[2] = one_hot(col == ((row & 1) << 6) + (((row & 15) >> 1) << 3) + (row >> 4))

    def reorder(i, v):
        return matmul(orders[i], v).astype(BF16)

    def pass_on(p):
        wait_all(mid, p, received.at[0, p])
        mid_out[p] = reorder(0, mid[p])
        exchange(1, p, mid_out, owned, along_cols, c)

    pass_on(0)

    loads[7].wait()
    flat[...] = jnp.zeros_like(flat)
    total = jnp.zeros((16, 256), F32)
    for q in range(15):
        flat[:, 0:15] = table_ref[q]
        total = total + (pltpu.roll(flat[...], 16 * q, 1) if q else flat[...])
    flat[...] = total

    def shift(h, carry):
        row = jnp.broadcast_to(flat[pl.ds(h, 1), :], (8, 256))
        for i in range(SIDE):
            moved = pltpu.roll(row, 137 + 16 * i, 1, stride=1, stride_axis=0)
            shifted[h, i * 8 : (i + 1) * 8] = moved[:, 0:128]
        return carry

    lax.fori_loop(0, 16, shift, 0, unroll=True)
    target = iota((1, 256), 1)
    lane = ((target >> 6) << 7) + (((target & 63) >> 3) << 4) + (target & 7)
    spread = one_hot(iota((512, 256), 0) == lane)

    def set_bias(q, carry):
        rest = jnp.concatenate([shifted[q * 4 + h] for h in range(4)], axis=1)
        parts = []
        for _ in range(3):
            parts.append(rest.astype(BF16))
            rest = rest - parts[-1].astype(F32)
        total = matmul(jnp.concatenate(parts, axis=0), spread)
        bias[q] = (total[0:64] + total[64:128] + total[128:192]) * LOG2E
        return carry

    lax.fori_loop(0, QUADS, set_bias, 0)
    loads[8].wait()

    head = iota((1, 128), 1) >> 5
    own_lanes = [head == h for h in range(4)]

    def attend(p):
        wait_all(owned, p, received.at[1, p])
        xg[...] = reorder(1, owned[p])

        def project(i, carry):
            lanes = pl.ds(pl.multiple_of(i * 256, 256), 256)
            qkv[:, lanes] = matmul(xg[...], wqkv[:, lanes]).astype(BF16)
            return carry

        lax.fori_loop(0, 6, project, 0, unroll=True)

        for t in range(GROUPS):
            rows = slice(t * 64, (t + 1) * 64)
            for q in range(QUADS):
                lanes = slice(q * 128, (q + 1) * 128)
                query = qkv[rows, lanes]
                keys = qkv[rows, 512 + q * 128 : 640 + q * 128]
                values = qkv[rows, 1024 + q * 128 : 1152 + q * 128]
                apart = jnp.concatenate([query * one_hot(own_lanes[h]) for h in range(4)], axis=0)
                scores = lax.dot_general(
                    keys, apart, (((1,), (1,)), ((), ())), preferred_element_type=F32
                )
                scores = scores * (32**-0.5 * LOG2E) + bias[q]
                powers = jnp.exp2(scores - jnp.max(scores, axis=0, keepdims=True))
                share = 1.0 / jnp.sum(powers, axis=0, keepdims=True)
                attention = (powers * share).astype(BF16)
                mixed = lax.dot_general(
                    attention, values, (((0,), (0,)), ((), ())), preferred_element_type=F32
                )
                total = jnp.where(own_lanes[0], mixed[0:64], 0.0)
                for h in range(1, 4):
                    total = jnp.where(own_lanes[h], mixed[h * 64 : (h + 1) * 64], total)
                context[rows, lanes] = total.astype(BF16)

        answers[p] = reorder(2, context[...])
        exchange(2, p, answers, mid_back, along_cols, c)

    def pass_back(p):
        wait_all(mid_back, p, received.at[2, p])
        mid_return[p] = reorder(0, mid_back[p])

        def send(k, carry):
            @pl.when(k != a)
            def _():
                pltpu.make_async_remote_copy(
                    src_ref=mid_return.at[p, block(k)],
                    dst_ref=returned.at[p, block(a)],
                    send_sem=sent.at[3, p],
                    recv_sem=received.at[3, p],
                    device_id=(k * SIDE + m, c),
                    device_id_type=MESH,
                ).start()

            return carry

        lax.fori_loop(0, SIDE, send, 0)
        returned[p, block(a)] = mid_return[p, block(a)]

    def step(i, carry):
        @pl.when(i < PARTS)
        def _():
            pass_on(i)

        @pl.when(i <= PARTS)
        def _():
            attend(i - 1)

        @pl.when(i >= 2)
        def _():
            pass_back(i - 2)

        return carry

    lax.fori_loop(1, PARTS + 2, step, 0)
    loads[9].wait()
    for i in range(2):
        restore[i] = one_hot(iota((CELLS, PART), 1) == place_of(i == 0, iota((CELLS, 1), 0)))

    for copy in halos:
        copy.wait_send()

    def drain(p, carry):
        for stage, ref in enumerate((att, mid_out, answers)):
            wait_all(ref, p, sent.at[stage, p])
        return carry

    lax.fori_loop(0, PARTS, drain, 0)

    def finish(p, carry):
        wait_all(returned, p, received.at[3, p])
        f, kind = p % FORECASTS, p // FORECASTS
        total = conv[p].astype(F32) + matmul(returned[p], wo[...])
        placed = matmul(restore[kind], total.astype(BF16))

        @pl.when(kind == 0)
        def _():
            finished[f] = placed

        @pl.when(kind == 1)
        def _():
            out_ref[f] = (finished[f] + placed).astype(BF16).reshape(ROWS, COLS, WIDTH)

        return carry

    lax.fori_loop(0, PARTS, finish, 0)

    def drain_back(p, carry):
        wait_all(mid_return, p, sent.at[3, p])
        return carry

    lax.fori_loop(0, PARTS, drain_back, 0)


def on_device(
    atmosphere_variables,
    premix_gain_vector,
    expand_weight,
    depth_weight,
    depth_bias,
    project_weight,
    norm_attn,
    qkv_weight,
    out_weight,
    bias_table,
):
    whole = pl.BlockSpec(memory_space=pltpu.HBM)
    tile = (FORECASTS, ROWS, COLS, WIDTH)
    parts = pltpu.VMEM((PARTS, PART, WIDTH), BF16)
    return pl.pallas_call(
        kernel,
        out_shape=pltpu.VMEM(tile, BF16),
        in_specs=[whole] * 10,
        out_specs=pl.BlockSpec(memory_space=pltpu.VMEM),
        scratch_shapes=[
            pltpu.VMEM(tile, BF16),
            pltpu.VMEM((1, WIDTH), F32),
            pltpu.VMEM((WIDTH, INNER), BF16),
            pltpu.VMEM((3, 3, INNER), F32),
            pltpu.VMEM((1, INNER), F32),
            pltpu.VMEM((INNER, WIDTH), BF16),
            pltpu.VMEM((1, WIDTH), F32),
            pltpu.VMEM((WIDTH, 3 * WIDTH), BF16),
            pltpu.VMEM((WIDTH, WIDTH), BF16),
            pltpu.VMEM((15, 16, 15), F32),
            pltpu.VMEM((6, 16, WIDTH), BF16),
            pltpu.VMEM((2, FORECASTS, COLS, WIDTH), BF16),
            pltpu.VMEM((6, 16, WIDTH), BF16),
            pltpu.VMEM((CELLS, WIDTH), BF16),
            pltpu.VMEM((FORECASTS, ROWS + 2, PADDED, INNER), F32),
            pltpu.VMEM((CELLS, INNER), BF16),
            pltpu.VMEM((PART, INNER), BF16),
            parts,
            pltpu.VMEM((2, PART, CELLS), BF16),
            pltpu.VMEM((2, CELLS, PART), BF16),
            pltpu.VMEM((FORECASTS, CELLS, WIDTH), F32),
            *[parts] * 8,
            pltpu.VMEM((3, PART, PART), BF16),
            pltpu.VMEM((PART, WIDTH), BF16),
            pltpu.VMEM((PART, 3 * WIDTH), BF16),
            pltpu.VMEM((PART, WIDTH), BF16),
            pltpu.VMEM((16, 256), F32),
            pltpu.VMEM((16, MEMBERS, 128), F32),
            pltpu.VMEM((QUADS, MEMBERS, 256), F32),
            pltpu.SemaphoreType.DMA((11,)),
            pltpu.SemaphoreType.DMA((8,)),
            pltpu.SemaphoreType.DMA((8,)),
            pltpu.SemaphoreType.DMA((4, PARTS)),
            pltpu.SemaphoreType.DMA((4, PARTS)),
        ],
        compiler_params=pltpu.CompilerParams(
            collective_id=0, has_side_effects=True, vmem_limit_bytes=56 * 1024 * 1024
        ),
        name="maxvit_layer",
    )(
        atmosphere_variables,
        premix_gain_vector.reshape(1, WIDTH),
        expand_weight,
        depth_weight,
        depth_bias.reshape(1, INNER),
        project_weight,
        norm_attn.reshape(1, WIDTH),
        qkv_weight,
        out_weight,
        bias_table.transpose(1, 0, 2),
    )


def solution(mesh):
    return jax.shard_map(
        on_device,
        mesh=mesh,
        in_specs=(P(None, "rows", "cols", None), P(), P(), P(), P(), P(), P(), P(), P(), P()),
        out_specs=P(None, "rows", "cols", None),
        check_vma=False,
    )
```
